32 devices in a mesh: replica: 2 (over y), fsdp: 16 (over z, x, core).
Axes of the slice: x: 2, y: 2, z: 4, core: 2. Of those that a mesh axis runs over, the one named last changes fastest.
Arguments:
- grads: bfloat16 [2, 2, 1024, 8192], P('replica', None, 'fsdp'), may hold values from -6 to 6
- errors: float32 [2, 2, 1024, 8192], P('replica', None, 'fsdp'), may hold values from -4 to 4
- basis: float32 [8192, 2, 32], P('fsdp'), may hold values from -6 to 6
Outputs:
- new_errors: float32 [2, 2, 1024, 8192], P('replica', None, 'fsdp')
- left_factor: float32 [2, 1024, 32], P(None, 'fsdp')
- new_basis: float32 [8192, 2, 32], P('fsdp')
The draws below stay inside these ranges and needn't reach their ends.
All inputs are finite; a program needn't handle non-finite values.
Results may differ from the reference program's by a relative error of at most 0.0003.
Values sent between devices are 32-bit elements; how exact they have to be, the bound alone decides.
A program may use at most 64 MiB of HBM per device.

```python
import jax
import jax.numpy as jnp
from jax import lax

D = 8192
MROWS = 1024
RANK = 32
NMAT = 2
REPLICAS = 2


def strengthened(drawn, rng, source, target, blocks, factor):
    owner, partner = [(jnp.arange(drawn.shape[dim]) // (drawn.shape[dim] // blocks)).reshape([-1 if axis == dim else 1 for axis in range(drawn.ndim)]) for dim in (source, target)]
    chosen = jax.random.permutation(rng, blocks)[partner]
    strong = (owner == chosen) | (owner == (partner + blocks // 2) % blocks)
    return jnp.where(strong, factor * drawn, drawn)


def block_levels(own_key, dims, split, smallest, largest):
    def one(axis_at, shards_of):
        steps = jax.random.uniform(jax.random.fold_in(jax.random.fold_in(own_key, 6), axis_at), (shards_of,), jnp.float32, smallest / len(split), largest / len(split))
        return jnp.repeat(jnp.exp(steps), dims[axis_at] // shards_of).reshape((-1,) + (1,) * (len(dims) - axis_at - 1))

    factor_of = one(*split[0])
    for cut in split[1:]:
        factor_of = factor_of * one(*cut)
    return factor_of


def bell_draw(stream_key, dims, width, most, pieces=(), held_as=jnp.bfloat16):
    values = width * jax.random.normal(stream_key, dims, jnp.float32)
    if pieces:
        values = values * block_levels(stream_key, dims, pieces, -0.22, 0.18)
    return jnp.clip(values, -most, most).astype(held_as)


def gaussian_with(stream_key, shape, deviation, most, split, heavy, dtype=jnp.bfloat16):
    drawn = deviation * jax.random.normal(stream_key, shape, jnp.float32)
    if split:
        drawn = drawn * block_levels(stream_key, shape, split, -0.22, 0.18)
    return jnp.clip(strengthened(drawn, jax.random.fold_in(stream_key, 3), *heavy), -most, most).astype(dtype)


def setup_inputs(seed: int = 0) -> dict:
    keys = jax.random.split(jax.random.key(seed), 4)
    grads = gaussian_with(keys[0], (REPLICAS, NMAT, MROWS, D), 1.0, 6.0, ((0, 2), (2, 16)), (2, 3, 16, 2.0))
    errors = bell_draw(keys[1], (REPLICAS, NMAT, MROWS, D), 0.3, 4.0, ((0, 2), (2, 16)), jnp.float32)
    basis = bell_draw(keys[2], (D, NMAT, RANK), 1.0, 6.0, ((0, 16),), jnp.float32)
    return {"grads": grads, "errors": errors, "basis": basis}


def orthonormal(factor):
    gram = jnp.einsum('mrk,mrl->mkl', factor, factor, precision=lax.Precision.HIGHEST)
    chol = jnp.linalg.cholesky(gram)

    def solve_one(lower, block):
        return jax.scipy.linalg.solve_triangular(lower, block.T, lower=True).T
    return jax.vmap(solve_one)(chol, factor)

def reference(grads, errors, basis):
    highest = lax.Precision.HIGHEST
    merged = grads.astype(jnp.float32) + errors
    factor = jnp.einsum('amrd,dmk->mrk', merged, basis, precision=highest) / REPLICAS
    left_factor = orthonormal(factor)
    new_basis = jnp.einsum('amrd,mrk->dmk', merged, left_factor, precision=highest) / REPLICAS
    approx = jnp.einsum('mrk,dmk->mrd', left_factor, new_basis, precision=highest)
    new_errors = merged - approx[None]
    return (new_errors, left_factor, new_basis)
```

```python
import functools

import jax
import jax.numpy as jnp
from jax import lax
from jax.experimental import pallas as pl
from jax.experimental.pallas import tpu as pltpu
from jax.sharding import PartitionSpec as P

MESH = pl.DeviceIdType.MESH
F32, BF16 = jnp.float32, jnp.bfloat16
TILE = 512
LANES = 128
NT = (((1,), (1,)), ((), ()))
NN = (((1,), (0,)), ((), ()))
TN = (((0,), (0,)), ((), ()))


def split(x):
    high = x.astype(BF16)
    return high, (x - high.astype(F32)).astype(BF16)


def dot32(a, b, dims):
    (ca,), (cb,) = dims[0]
    ah, al = split(a)
    bh, bl = split(b)
    left = jnp.concatenate([ah, ah, al], axis=ca)
    right = jnp.concatenate([bh, bl, bh], axis=cb)
    return lax.dot_general(left, right, dims, preferred_element_type=F32)


def log2(n):
    return n.bit_length() - 1


def orders(nb, nr):
    core = [("fsdp", 0)]
    near = [("fsdp", 1)]
    far = [("fsdp", b) for b in range(2, nb)]
    across = [("replica", b) for b in range(nr)]
    reduce_parts = [
        (0, 24, core + near + across + far),
        (24, 48, core + across + far + near),
        (48, 64, core + far + near + across),
    ]
    back = far[::-1]
    gather_parts = [back + near + core, near + back + core]
    return reduce_parts, gather_parts


def exchange(
    n, replicas, grads, errors, basis, total, left_t, own_basis, inverse,
    held, g_buf, e_buf, mhl, acc, ft, ft_in, z, z_in, gram, gram_in,
    load_sem, a_send, a_recv, f_send, f_recv, s_send, s_recv, m_send, m_recv, b_send, b_recv,
):
    nb, nr = log2(n), log2(replicas)
    reduce_parts, gather_parts = orders(nb, nr)
    rank = basis.shape[0] // 2
    width = basis.shape[1]
    rows = grads.shape[1]
    cols = grads.shape[2]
    y, f = lax.axis_index("replica"), lax.axis_index("fsdp")

    def bit_of(axis, bit):
        return lax.rem(lax.div(f if axis == "fsdp" else y, 1 << bit), 2)

    def partner(axis, bit):
        step = (1 - 2 * bit_of(axis, bit)) * (1 << bit)
        return (y, f + step) if axis == "fsdp" else (y + step, f)

    loads = [
        pltpu.make_async_copy(grads, g_buf, load_sem.at[0]),
        pltpu.make_async_copy(errors, e_buf, load_sem.at[1]),
    ]
    for load in loads:
        load.start()

    links = [("fsdp", b) for b in range(nb)] + [("replica", b) for b in range(nr)]
    barrier = pltpu.get_barrier_semaphore()
    for link in links:
        pl.semaphore_signal(barrier, inc=1, device_id=partner(*link), device_id_type=MESH)
    mine = tuple(bit_of("fsdp", b) for b in range(nb - 1, -1, -1))
    held[mine] = basis[...]
    pl.semaphore_wait(barrier, len(links))

    def gather_copy(part, step):
        done = [bit for _, bit in gather_parts[part][:step]]
        at = tuple(slice(None) if b in done else bit_of("fsdp", b) for b in range(nb - 1, -1, -1))
        at = at + (pl.ds(part * rank, rank), slice(None))
        return pltpu.make_async_remote_copy(
            src_ref=held.at[at], dst_ref=held.at[at],
            send_sem=a_send.at[part, step], recv_sem=a_recv.at[part, step],
            device_id=partner(*gather_parts[part][step]), device_id_type=MESH,
        )

    def factor_tile(part, shard):
        at = tuple(lax.rem(lax.div(shard, 1 << b), 2) for b in range(nb - 1, -1, -1))
        high, low = split(held[at + (pl.ds(part * rank, rank), slice(None))])
        here = pl.ds(pl.multiple_of(shard * width, width), width)
        acc[part] += lax.dot_general(
            jnp.concatenate([high, low], axis=0), mhl[part, :, here], NT, preferred_element_type=F32
        )

    def factor_step(part, step):
        done = [bit for _, bit in gather_parts[part][:step]]
        now = gather_parts[part][step][1]
        base = sum(
            ((1 - bit_of("fsdp", b)) if b == now else bit_of("fsdp", b)) * (1 << b)
            for b in range(nb) if b not in done
        )

        @pl.loop(0, 1 << step)
        def _(j):
            shard = base
            for i, b in enumerate(done):
                shard = shard + lax.rem(lax.div(j, 1 << i), 2) * (1 << b)
            factor_tile(part, shard)

    copies = [gather_copy(part, 0) for part in range(2)]
    for copy in copies:
        copy.start()
    acc[...] = jnp.zeros_like(acc)
    for load in loads:
        load.wait()

    @pl.loop(0, cols // TILE)
    def _(t):
        here = pl.ds(pl.multiple_of(t * TILE, TILE), TILE)
        for m in range(2):
            high, low = split(g_buf[m, :, here].astype(F32) + e_buf[m, :, here])
            mhl[m, 0:rows, here] = high
            mhl[m, rows : 2 * rows, here] = low

    for part in range(2):
        factor_tile(part, f)
    for step in range(nb):
        for copy in copies:
            copy.wait()
        if step + 1 < nb:
            copies = [gather_copy(part, step + 1) for part in range(2)]
            for copy in copies:
                copy.start()
        for part in range(2):
            factor_step(part, step)

    for m in range(2):
        whole = acc[m, 0:rank] + acc[m, rank : 2 * rank]
        one = whole[:, 0:rows] + whole[:, rows : 2 * rows]
        ft[0, m * rank : (m + 1) * rank] = jnp.concatenate([one, one], axis=1)
    for b in range(nr):
        copy = pltpu.make_async_remote_copy(
            src_ref=ft.at[b], dst_ref=ft_in.at[b], send_sem=f_send.at[b], recv_sem=f_recv.at[b],
            device_id=partner("replica", b), device_id_type=MESH,
        )
        copy.start()
        copy.wait()
        ft[b + 1] = ft[b] + ft_in[b]
    factor = ft[nr] * (1.0 / replicas)
    f_high, f_low = split(factor)
    weights = [
        jnp.concatenate([f_high[m * rank : (m + 1) * rank], f_low[m * rank : (m + 1) * rank]], axis=0)
        for m in range(2)
    ]

    def term(start, count):
        @pl.loop(0, count // TILE)
        def _(t):
            here = pl.ds(pl.multiple_of(start + t * TILE, TILE), TILE)
            for m in range(2):
                out = lax.dot_general(weights[m], mhl[m, :, here], NN, preferred_element_type=F32)
                z[m * rank : (m + 1) * rank, here] = out[0:rank] + out[rank : 2 * rank]

    nsteps = nb + nr
    half = cols // 2
    core = bit_of("fsdp", 0)
    term((1 - core) * half, half)
    starts = [0 for _ in reduce_parts]
    sizes = [cols for _ in reduce_parts]
    history = [[] for _ in reduce_parts]
    offset = 0
    for step in range(nsteps):
        pieces = []
        size = sizes[0]
        cut = size > LANES
        part_size = size // 2 if cut else size
        for p, (low, high, order) in enumerate(reduce_parts):
            link = order[step]
            bit = bit_of(*link)
            away = starts[p] + (1 - bit) * part_size if cut else starts[p]
            keep = starts[p] + bit * part_size if cut else starts[p]
            away = pl.multiple_of(away, LANES)
            copy = pltpu.make_async_remote_copy(
                src_ref=z.at[pl.ds(low, high - low), pl.ds(away, part_size)],
                dst_ref=z_in.at[pl.ds(low, high - low), pl.ds(offset, part_size)],
                send_sem=s_send.at[p, step], recv_sem=s_recv.at[p, step],
                device_id=partner(*link), device_id_type=MESH,
            )
            copy.start()
            history[p].append((link, bit, cut))
            pieces.append((copy, keep))
        if step == 0:
            term(core * half, half)
            product = lax.dot_general(
                factor, jnp.concatenate([factor, factor], axis=0), NT,
                precision=lax.Precision.HIGHEST, preferred_element_type=F32,
            ) * 0.5
            lane = lax.broadcasted_iota(jnp.int32, (rank, LANES), 1)
            gram[0] = jnp.where(lane < rank, product[0:rank], product[rank : 2 * rank])
        link = reduce_parts[0][2][step]
        g_copy = None
        if link[0] == "fsdp":
            g_copy = pltpu.make_async_remote_copy(
                src_ref=gram.at[step], dst_ref=gram_in.at[step],
                send_sem=m_send.at[step], recv_sem=m_recv.at[step],
                device_id=partner(*link), device_id_type=MESH,
            )
            g_copy.start()
        for p, (low, high, order) in enumerate(reduce_parts):
            copy, keep = pieces[p]
            copy.wait()
            here = pl.ds(pl.multiple_of(keep, LANES), part_size)
            z[low:high, here] = z[low:high, here] + z_in[low:high, offset : offset + part_size]
            starts[p], sizes[p] = keep, part_size
        if g_copy is not None:
            g_copy.wait()
            gram[step + 1] = gram[step] + gram_in[step]
        else:
            gram[step + 1] = gram[step]
        offset += part_size

    for p, (low, high, _) in enumerate(reduce_parts):
        here = pl.ds(pl.multiple_of(starts[p], LANES), sizes[p])
        total[low:high, here] = z[low:high, here]

    def back(step):
        out = []
        for p, (low, high, _) in enumerate(reduce_parts):
            link, bit, cut = history[p][step]
            if not cut:
                continue
            at = (pl.ds(low, high - low), pl.ds(pl.multiple_of(starts[p], LANES), sizes[p]))
            copy = pltpu.make_async_remote_copy(
                src_ref=total.at[at], dst_ref=total.at[at],
                send_sem=b_send.at[p, step], recv_sem=b_recv.at[p, step],
                device_id=partner(*link), device_id_type=MESH,
            )
            copy.start()
            out.append(copy)
            starts[p] = starts[p] - bit * sizes[p]
            sizes[p] = 2 * sizes[p]
        return out

    copies = back(nsteps - 1)

    row = lax.broadcasted_iota(jnp.int32, (rank, LANES), 0)
    lane = lax.broadcasted_iota(jnp.int32, (rank, LANES), 1)
    first = lax.rem(lane, 2 * rank) < rank
    work = jnp.where(lane < 2 * rank, gram[nsteps], jnp.where(lax.rem(lane, rank) == row, 1.0, 0.0))
    for j in range(rank):
        column = jnp.where(first, work[:, j : j + 1], work[:, rank + j : rank + j + 1])
        top = work[j : j + 1, :] / column[j : j + 1, :]
        work = jnp.where(row > j, work - column * top, work)
    pivots = [
        jnp.sum(jnp.where(lane == row + m * rank, work, 0.0), axis=1, keepdims=True) for m in range(2)
    ]
    scaled = work / jnp.sqrt(jnp.where(first, pivots[0], pivots[1]))
    inv = [scaled[:, (2 + m) * rank : (3 + m) * rank] for m in range(2)]
    for m in range(2):
        inverse[m * rank : (m + 1) * rank] = inv[m]
        left_t[m * rank : (m + 1) * rank] = lax.dot_general(
            inv[m], factor[m * rank : (m + 1) * rank, 0:rows], NN,
            precision=lax.Precision.HIGHEST, preferred_element_type=F32,
        )

    for step in range(nsteps - 1, -1, -1):
        for copy in copies:
            copy.wait()
        if step > 0:
            copies = back(step - 1)
    own = pl.ds(pl.multiple_of(f * width, LANES), width)
    for m in range(2):
        at = slice(m * rank, (m + 1) * rank)
        own_basis[at] = dot32(inv[m], total[at, own], NN) * (1.0 / replicas)


def finish(replicas, grads, errors, total, left_t, inverse, out):
    rank = total.shape[0] // 2
    for m in range(2):
        at = slice(m * rank, (m + 1) * rank)
        basis = dot32(inverse[at], total[at], NN) * (1.0 / replicas)
        approx = dot32(left_t[at], basis, TN)
        out[m] = grads[m].astype(F32) + errors[m] - approx


def solution(mesh):
    n, replicas = mesh.shape["fsdp"], mesh.shape["replica"]
    nb, nr = log2(n), log2(replicas)
    steps = nb + nr

    def shards(grads, errors, basis):
        _, nmat, rows, cols = grads.shape
        width, _, rank = basis.shape
        grads, errors = grads[0], errors[0]
        basis_t = jnp.transpose(basis, (1, 2, 0)).reshape(nmat * rank, width)
        full = nmat * rank
        vmem = pl.BlockSpec(memory_space=pltpu.VMEM)
        hbm = pl.BlockSpec(memory_space=pl.ANY)
        dma = pltpu.SemaphoreType.DMA
        total, left_t, own_basis, inverse = pl.pallas_call(
            functools.partial(exchange, n, replicas),
            out_shape=[
                jax.ShapeDtypeStruct((full, cols), F32),
                jax.ShapeDtypeStruct((full, rows), F32),
                jax.ShapeDtypeStruct((full, width), F32),
                jax.ShapeDtypeStruct((full, rank), F32),
            ],
            in_specs=[hbm, hbm, vmem],
            out_specs=[vmem] * 4,
            scratch_shapes=[
                pltpu.VMEM((2,) * nb + (full, width), F32),
                pltpu.VMEM((nmat, rows, cols), BF16),
                pltpu.VMEM((nmat, rows, cols), F32),
                pltpu.VMEM((nmat, 2 * rows, cols), BF16),
                pltpu.VMEM((nmat, 2 * rank, 2 * rows), F32),
                pltpu.VMEM((nr + 1, full, 2 * rows), F32),
                pltpu.VMEM((nr, full, 2 * rows), F32),
                pltpu.VMEM((full, cols), F32),
                pltpu.VMEM((full, cols + LANES * steps), F32),
                pltpu.VMEM((steps + 1, rank, LANES), F32),
                pltpu.VMEM((steps, rank, LANES), F32),
                dma((2,)),
                dma((2, nb)), dma((2, nb)),
                dma((nr,)), dma((nr,)),
                dma((3, steps)), dma((3, steps)),
                dma((steps,)), dma((steps,)),
                dma((3, steps)), dma((3, steps)),
            ],
            compiler_params=pltpu.CompilerParams(
                collective_id=0, has_side_effects=True, vmem_limit_bytes=40 * 1024 * 1024
            ),
        )(grads, errors, basis_t)

        block = 1024
        whole = lambda a: pl.BlockSpec(a.shape, lambda i: (0, 0))
        new_errors = pl.pallas_call(
            functools.partial(finish, replicas),
            grid=(cols // block,),
            out_shape=jax.ShapeDtypeStruct((nmat, rows, cols), F32),
            in_specs=[
                pl.BlockSpec((nmat, rows, block), lambda i: (0, 0, i)),
                pl.BlockSpec((nmat, rows, block), lambda i: (0, 0, i)),
                pl.BlockSpec((full, block), lambda i: (0, i)),
                whole(left_t),
                whole(inverse),
            ],
            out_specs=pl.BlockSpec((nmat, rows, block), lambda i: (0, 0, i)),
            compiler_params=pltpu.CompilerParams(vmem_limit_bytes=32 * 1024 * 1024),
        )(grads, errors, total, left_t, inverse)
        left = jnp.transpose(left_t.reshape(nmat, rank, rows), (0, 2, 1))
        new_basis = jnp.transpose(own_basis.reshape(nmat, rank, width), (2, 0, 1))
        return (new_errors[None], left, new_basis)

    in_specs = (
        P("replica", None, "fsdp", None),
        P("replica", None, "fsdp", None),
        P("fsdp", None, None),
    )
    out_specs = (P("replica", None, "fsdp", None), P(None, "fsdp", None), P("fsdp", None, None))
    return jax.shard_map(shards, mesh=mesh, in_specs=in_specs, out_specs=out_specs, check_vma=False)
```

```python
import functools

import jax
import jax.numpy as jnp
from jax import lax
from jax.experimental import pallas as pl
from jax.experimental.pallas import tpu as pltpu
from jax.sharding import PartitionSpec as P

MESH = pl.DeviceIdType.MESH
F32, BF16 = jnp.float32, jnp.bfloat16
TILE = 512
LANES = 128
NT = (((1,), (1,)), ((), ()))
NN = (((1,), (0,)), ((), ()))
TN = (((0,), (0,)), ((), ()))


def split(x):
    high = x.astype(BF16)
    return high, (x - high.astype(F32)).astype(BF16)


def dot32(a, b, dims):
    (ca,), (cb,) = dims[0]
    ah, al = split(a)
    bh, bl = split(b)
    left = jnp.concatenate([ah, ah, al], axis=ca)
    right = jnp.concatenate([bh, bl, bh], axis=cb)
    return lax.dot_general(left, right, dims, preferred_element_type=F32)


def log2(n):
    return n.bit_length() - 1


def orders(nb, nr):
    core = [("fsdp", 0)]
    near = [("fsdp", 1)]
    far = [("fsdp", b) for b in range(2, nb)]
    across = [("replica", b) for b in range(nr)]
    first = core + near + across + far
    second = core + across + far + near
    third = core + far + near + across
    reduce_parts = [
        (0, 8, first), (8, 24, first), (24, 32, third),
        (32, 40, third), (40, 48, second), (48, 64, second),
    ]
    back = far[::-1]
    gather_parts = [back + near + core, near + back + core]
    return reduce_parts, gather_parts


def exchange(
    n, replicas, grads, errors, basis, total, left_t, own_basis, folded,
    held, g_buf, e_buf, mhl, acc, ft, ft_in, z, z_in, gram, gram_in,
    load_sem, a_send, a_recv, f_send, f_recv, s_send, s_recv, m_send, m_recv, b_send, b_recv,
):
    nb, nr = log2(n), log2(replicas)
    reduce_parts, gather_parts = orders(nb, nr)
    rank = basis.shape[0] // 2
    width = basis.shape[1]
    rows = grads.shape[1]
    cols = grads.shape[2]
    y, f = lax.axis_index("replica"), lax.axis_index("fsdp")

    def bit_of(axis, bit):
        return lax.rem(lax.div(f if axis == "fsdp" else y, 1 << bit), 2)

    def partner(axis, bit):
        step = (1 - 2 * bit_of(axis, bit)) * (1 << bit)
        return (y, f + step) if axis == "fsdp" else (y + step, f)

    loads = [
        pltpu.make_async_copy(grads, g_buf, load_sem.at[0]),
        pltpu.make_async_copy(errors, e_buf, load_sem.at[1]),
    ]
    for load in loads:
        load.start()

    links = [("fsdp", b) for b in range(nb)] + [("replica", b) for b in range(nr)]
    barrier = pltpu.get_barrier_semaphore()
    for link in links:
        pl.semaphore_signal(barrier, inc=1, device_id=partner(*link), device_id_type=MESH)
    mine = tuple(bit_of("fsdp", b) for b in range(nb - 1, -1, -1))
    held[mine] = basis[...]
    pl.semaphore_wait(barrier, len(links))

    def gather_copy(part, step):
        done = [bit for _, bit in gather_parts[part][:step]]
        at = tuple(slice(None) if b in done else bit_of("fsdp", b) for b in range(nb - 1, -1, -1))
        at = at + (pl.ds(part * rank, rank), slice(None))
        return pltpu.make_async_remote_copy(
            src_ref=held.at[at], dst_ref=held.at[at],
            send_sem=a_send.at[part, step], recv_sem=a_recv.at[part, step],
            device_id=partner(*gather_parts[part][step]), device_id_type=MESH,
        )

    def factor_tile(part, shard):
        at = tuple(lax.rem(lax.div(shard, 1 << b), 2) for b in range(nb - 1, -1, -1))
        high, low = split(held[at + (pl.ds(part * rank, rank), slice(None))])
        here = pl.ds(pl.multiple_of(shard * width, width), width)
        acc[part] += lax.dot_general(
            jnp.concatenate([high, low], axis=0), mhl[part, :, here], NT, preferred_element_type=F32
        )

    def factor_step(part, step):
        done = [bit for _, bit in gather_parts[part][:step]]
        now = gather_parts[part][step][1]
        base = sum(
            ((1 - bit_of("fsdp", b)) if b == now else bit_of("fsdp", b)) * (1 << b)
            for b in range(nb) if b not in done
        )

        @pl.loop(0, 1 << step)
        def _(j):
            shard = base
            for i, b in enumerate(done):
                shard = shard + lax.rem(lax.div(j, 1 << i), 2) * (1 << b)
            factor_tile(part, shard)

    copies = [gather_copy(part, 0) for part in range(2)]
    for copy in copies:
        copy.start()
    acc[...] = jnp.zeros_like(acc)
    for load in loads:
        load.wait()

    @pl.loop(0, cols // TILE)
    def _(t):
        here = pl.ds(pl.multiple_of(t * TILE, TILE), TILE)
        for m in range(2):
            high, low = split(g_buf[m, :, here].astype(F32) + e_buf[m, :, here])
            mhl[m, 0:rows, here] = high
            mhl[m, rows : 2 * rows, here] = low

    for part in range(2):
        factor_tile(part, f)
    for step in range(nb):
        for part in range(2):
            copies[part].wait()
            if step + 1 < nb:
                copies[part] = gather_copy(part, step + 1)
                copies[part].start()
        for part in range(2):
            factor_step(part, step)

    for m in range(2):
        whole = acc[m, 0:rank] + acc[m, rank : 2 * rank]
        one = whole[:, 0:rows] + whole[:, rows : 2 * rows]
        ft[0, m * rank : (m + 1) * rank] = jnp.concatenate([one, one], axis=1)
    for b in range(nr):
        copy = pltpu.make_async_remote_copy(
            src_ref=ft.at[b], dst_ref=ft_in.at[b], send_sem=f_send.at[b], recv_sem=f_recv.at[b],
            device_id=partner("replica", b), device_id_type=MESH,
        )
        copy.start()
        copy.wait()
        ft[b + 1] = ft[b] + ft_in[b]
    factor = ft[nr] * (1.0 / replicas)
    f_high, f_low = split(factor)
    weights = [
        jnp.concatenate([f_high[m * rank : (m + 1) * rank], f_low[m * rank : (m + 1) * rank]], axis=0)
        for m in range(2)
    ]

    def term(m, start, count):
        @pl.loop(0, count // TILE)
        def _(t):
            here = pl.ds(pl.multiple_of(start + t * TILE, TILE), TILE)
            out = lax.dot_general(weights[m], mhl[m, :, here], NN, preferred_element_type=F32)
            z[m * rank : (m + 1) * rank, here] = out[0:rank] + out[rank : 2 * rank]

    nsteps = nb + nr
    half = cols // 2
    core = bit_of("fsdp", 0)
    parts = range(len(reduce_parts))
    cuts, sizes, offsets = [], [cols], [0]
    for step in range(nsteps):
        cuts.append(sizes[-1] > LANES)
        sizes.append(sizes[-1] // 2 if cuts[-1] else sizes[-1])
        offsets.append(offsets[-1] + sizes[-1])
    starts = [[0] for _ in parts]

    def send(p, step):
        low, high, order = reduce_parts[p]
        bit, size, start = bit_of(*order[step]), sizes[step + 1], starts[p][step]
        away = start + (1 - bit) * size if cuts[step] else start
        starts[p].append(start + bit * size if cuts[step] else start)
        copy = pltpu.make_async_remote_copy(
            src_ref=z.at[pl.ds(low, high - low), pl.ds(pl.multiple_of(away, LANES), size)],
            dst_ref=z_in.at[pl.ds(low, high - low), pl.ds(offsets[step], size)],
            send_sem=s_send.at[p, step], recv_sem=s_recv.at[p, step],
            device_id=partner(*order[step]), device_id_type=MESH,
        )
        copy.start()
        return copy

    def gram_copy(step):
        link = reduce_parts[0][2][step]
        if link[0] != "fsdp":
            return None
        copy = pltpu.make_async_remote_copy(
            src_ref=gram.at[step], dst_ref=gram_in.at[step],
            send_sem=m_send.at[step], recv_sem=m_recv.at[step],
            device_id=partner(*link), device_id_type=MESH,
        )
        copy.start()
        return copy

    copies = []
    for m in range(2):
        term(m, (1 - core) * half, half)
        copies += [send(p, 0) for p in parts if reduce_parts[p][0] // rank == m]
    product = lax.dot_general(
        factor, jnp.concatenate([factor, factor], axis=0), NT,
        precision=lax.Precision.HIGHEST, preferred_element_type=F32,
    ) * 0.5
    lane = lax.broadcasted_iota(jnp.int32, (rank, LANES), 1)
    gram[0] = jnp.where(lane < rank, product[0:rank], product[rank : 2 * rank])
    g_copy = gram_copy(0)
    for m in range(2):
        term(m, core * half, half)
    for step in range(nsteps):
        size, offset = sizes[step + 1], offsets[step]
        for p in parts:
            low, high, _ = reduce_parts[p]
            copies[p].wait()
            here = pl.ds(pl.multiple_of(starts[p][step + 1], LANES), size)
            added = z[low:high, here] + z_in[low:high, offset : offset + size]
            if step + 1 < nsteps:
                z[low:high, here] = added
                copies[p] = send(p, step + 1)
            else:
                total[low:high, here] = added
        if g_copy is not None:
            g_copy.wait()
            gram[step + 1] = gram[step] + gram_in[step]
        else:
            gram[step + 1] = gram[step]
        g_copy = gram_copy(step + 1) if step + 1 < nsteps else None

    def back(p, step):
        low, high, order = reduce_parts[p]
        if not cuts[step]:
            return None
        at = (pl.ds(low, high - low), pl.ds(pl.multiple_of(starts[p][step + 1], LANES), sizes[step + 1]))
        copy = pltpu.make_async_remote_copy(
            src_ref=total.at[at], dst_ref=total.at[at],
            send_sem=b_send.at[p, step], recv_sem=b_recv.at[p, step],
            device_id=partner(*order[step]), device_id_type=MESH,
        )
        copy.start()
        return copy

    copies = [back(p, nsteps - 1) for p in parts]

    row = lax.broadcasted_iota(jnp.int32, (rank, LANES), 0)
    lane = lax.broadcasted_iota(jnp.int32, (rank, LANES), 1)
    first = lax.rem(lane, 2 * rank) < rank
    work = jnp.where(lane < 2 * rank, gram[nsteps], jnp.where(lax.rem(lane, rank) == row, 1.0, 0.0))
    for j in range(rank):
        column = jnp.where(first, work[:, j : j + 1], work[:, rank + j : rank + j + 1])
        top = work[j : j + 1, :] / column[j : j + 1, :]
        work = jnp.where(row > j, work - column * top, work)
    pivots = [
        jnp.sum(jnp.where(lane == row + m * rank, work, 0.0), axis=1, keepdims=True) for m in range(2)
    ]
    scaled = work / jnp.sqrt(jnp.where(first, pivots[0], pivots[1]))
    inv = [scaled[:, (2 + m) * rank : (3 + m) * rank] for m in range(2)]
    for m in range(2):
        solved = lax.dot_general(
            inv[m], factor[m * rank : (m + 1) * rank, 0:rows], NN,
            precision=lax.Precision.HIGHEST, preferred_element_type=F32,
        )
        left_t[m * rank : (m + 1) * rank] = solved
        folded[m * rank : (m + 1) * rank] = lax.dot_general(
            inv[m], solved, TN, precision=lax.Precision.HIGHEST, preferred_element_type=F32
        ) * (1.0 / replicas)

    for step in range(nsteps - 1, -1, -1):
        for p in parts:
            if copies[p] is not None:
                copies[p].wait()
            if step > 0:
                copies[p] = back(p, step - 1)
    own = pl.ds(pl.multiple_of(f * width, LANES), width)
    for m in range(2):
        at = slice(m * rank, (m + 1) * rank)
        own_basis[at] = dot32(inv[m], total[at, own], NN) * (1.0 / replicas)


def finish(grads, errors, total, folded, out):
    rank = total.shape[0] // 2
    for m in range(2):
        at = slice(m * rank, (m + 1) * rank)
        out[m] = grads[m].astype(F32) + errors[m] - dot32(folded[at], total[at], TN)


def solution(mesh):
    n, replicas = mesh.shape["fsdp"], mesh.shape["replica"]
    nb, nr = log2(n), log2(replicas)
    steps = nb + nr

    def shards(grads, errors, basis):
        _, nmat, rows, cols = grads.shape
        width, _, rank = basis.shape
        grads, errors = grads[0], errors[0]
        basis_t = jnp.transpose(basis, (1, 2, 0)).reshape(nmat * rank, width)
        full = nmat * rank
        vmem = pl.BlockSpec(memory_space=pltpu.VMEM)
        hbm = pl.BlockSpec(memory_space=pl.ANY)
        dma = pltpu.SemaphoreType.DMA
        total, left_t, own_basis, folded = pl.pallas_call(
            functools.partial(exchange, n, replicas),
            out_shape=[
                jax.ShapeDtypeStruct((full, cols), F32),
                jax.ShapeDtypeStruct((full, rows), F32),
                jax.ShapeDtypeStruct((full, width), F32),
                jax.ShapeDtypeStruct((full, rows), F32),
            ],
            in_specs=[hbm, hbm, vmem],
            out_specs=[vmem] * 4,
            scratch_shapes=[
                pltpu.VMEM((2,) * nb + (full, width), F32),
                pltpu.VMEM((nmat, rows, cols), BF16),
                pltpu.VMEM((nmat, rows, cols), F32),
                pltpu.VMEM((nmat, 2 * rows, cols), BF16),
                pltpu.VMEM((nmat, 2 * rank, 2 * rows), F32),
                pltpu.VMEM((nr + 1, full, 2 * rows), F32),
                pltpu.VMEM((nr, full, 2 * rows), F32),
                pltpu.VMEM((full, cols), F32),
                pltpu.VMEM((full, cols + LANES * steps), F32),
                pltpu.VMEM((steps + 1, rank, LANES), F32),
                pltpu.VMEM((steps, rank, LANES), F32),
                dma((2,)),
                dma((2, nb)), dma((2, nb)),
                dma((nr,)), dma((nr,)),
                dma((6, steps)), dma((6, steps)),
                dma((steps,)), dma((steps,)),
                dma((6, steps)), dma((6, steps)),
            ],
            compiler_params=pltpu.CompilerParams(
                collective_id=0, has_side_effects=True, vmem_limit_bytes=60 * 1024 * 1024
            ),
        )(grads, errors, basis_t)

        block = 1024
        whole = lambda a: pl.BlockSpec(a.shape, lambda i: (0, 0))
        new_errors = pl.pallas_call(
            finish,
            grid=(cols // block,),
            out_shape=jax.ShapeDtypeStruct((nmat, rows, cols), F32),
            in_specs=[
                pl.BlockSpec((nmat, rows, block), lambda i: (0, 0, i)),
                pl.BlockSpec((nmat, rows, block), lambda i: (0, 0, i)),
                pl.BlockSpec((full, block), lambda i: (0, i)),
                whole(folded),
            ],
            out_specs=pl.BlockSpec((nmat, rows, block), lambda i: (0, 0, i)),
            compiler_params=pltpu.CompilerParams(vmem_limit_bytes=60 * 1024 * 1024),
        )(grads, errors, total, folded)
        left = jnp.transpose(left_t.reshape(nmat, rank, rows), (0, 2, 1))
        new_basis = jnp.transpose(own_basis.reshape(nmat, rank, width), (2, 0, 1))
        return (new_errors[None], left, new_basis)

    in_specs = (
        P("replica", None, "fsdp", None),
        P("replica", None, "fsdp", None),
        P("fsdp", None, None),
    )
    out_specs = (P("replica", None, "fsdp", None), P(None, "fsdp", None), P("fsdp", None, None))
    return jax.shard_map(shards, mesh=mesh, in_specs=in_specs, out_specs=out_specs, check_vma=False)
```

```python
import functools

import jax
import jax.numpy as jnp
from jax import lax
from jax.experimental import pallas as pl
from jax.experimental.pallas import tpu as pltpu
from jax.sharding import PartitionSpec as P

MESH = pl.DeviceIdType.MESH
F32, BF16 = jnp.float32, jnp.bfloat16
TILE = 512
LANES = 128
NT = (((1,), (1,)), ((), ()))
NN = (((1,), (0,)), ((), ()))
TN = (((0,), (0,)), ((), ()))


def split(x):
    high = x.astype(BF16)
    return high, (x - high.astype(F32)).astype(BF16)


def dot32(a, b, dims):
    (ca,), (cb,) = dims[0]
    ah, al = split(a)
    bh, bl = split(b)
    left = jnp.concatenate([ah, ah, al], axis=ca)
    right = jnp.concatenate([bh, bl, bh], axis=cb)
    return lax.dot_general(left, right, dims, preferred_element_type=F32)


def log2(n):
    return n.bit_length() - 1


def plan(nb, nr, share):
    core, near = [("fsdp", 0)], [("fsdp", 1)]
    far = [("fsdp", b) for b in range(2, nb)]
    across = [("replica", b) for b in range(nr)]
    plane_first = [core, near + across, far]
    far_first = [core, far, near + across]
    reduce_parts = [
        (0, 16, plane_first), (16, 32, plane_first), (32, 40, plane_first),
        (40, 48, far_first), (48, 64, far_first),
    ]
    plane = near + across if share else near
    gather_parts = [(0, 40, [far, plane, core]), (40, 64, [plane, far, core])]
    return reduce_parts, gather_parts


def layout(nb, nr, cols):
    out = []
    for _, _, stages in plan(nb, nr, False)[0]:
        cuts, sizes, offsets = [], [cols], [0]
        for stage in stages:
            members = 1 << len(stage)
            cuts.append(sizes[-1] // members >= LANES)
            sizes.append(sizes[-1] // members if cuts[-1] else sizes[-1])
            offsets.append(offsets[-1] + (members - cuts[-1]) * sizes[-1])
        out.append((cuts, sizes, offsets))
    return out


def exchange(
    n, replicas, share, grads, errors, basis, total, left_t, own_basis, folded,
    held, g_buf, e_buf, mhl, acc, ft, ft_in, z, z_in, gram, gram_in,
    load_sem, a_send, a_recv, f_send, f_recv, s_send, s_recv, m_send, m_recv, b_send, b_recv,
):
    nb, nr = log2(n), log2(replicas)
    reduce_parts, gather_parts = plan(nb, nr, share)
    rank = basis.shape[0] // 2
    width = basis.shape[1]
    rows = grads.shape[1]
    cols = grads.shape[2]
    y, f = lax.axis_index("replica"), lax.axis_index("fsdp")

    def bit_of(link):
        return lax.rem(lax.div(f if link[0] == "fsdp" else y, 1 << link[1]), 2)

    def index_of(stage, mask=0):
        total_index = 0
        for i, link in enumerate(stage):
            own = bit_of(link)
            total_index = total_index + (1 - own if mask >> i & 1 else own) * (1 << i)
        return total_index

    def partner(stage, mask):
        there = {"replica": y, "fsdp": f}
        for i, link in enumerate(stage):
            if mask >> i & 1:
                there[link[0]] = there[link[0]] + (1 - 2 * bit_of(link)) * (1 << link[1])
        return (there["replica"], there["fsdp"])

    def masks(stage):
        return range(1, 1 << len(stage))

    loads = [
        pltpu.make_async_copy(grads, g_buf, load_sem.at[0]),
        pltpu.make_async_copy(errors, e_buf, load_sem.at[1]),
    ]
    for load in loads:
        load.start()

    barrier = pltpu.get_barrier_semaphore()
    peers = [(stage, mask) for stage in reduce_parts[0][2] for mask in masks(stage)]
    for stage, mask in peers:
        pl.semaphore_signal(barrier, inc=1, device_id=partner(stage, mask), device_id_type=MESH)
    held_links = [("fsdp", b) for b in range(nb - 1, -1, -1)]
    if share:
        held_links += [("replica", b) for b in range(nr - 1, -1, -1)]
    piece = held.shape[-1]
    mine = tuple(bit_of(link) for link in held_links)
    first_column = sum(bit_of(link) * (1 << link[1]) for link in held_links if link[0] == "replica") * piece
    if share:
        held[mine] = basis[:, pl.ds(pl.multiple_of(first_column, LANES), piece)]
    else:
        held[mine] = basis[...]
    pl.semaphore_wait(barrier, len(peers))

    def gather(part, step):
        low, high, stages = gather_parts[part]
        done = [link for stage in stages[:step] for link in stage]
        at = tuple(slice(None) if link in done else bit_of(link) for link in held_links)
        at = at + (pl.ds(low, high - low), slice(None))
        out = []
        for mask in masks(stages[step]):
            copy = pltpu.make_async_remote_copy(
                src_ref=held.at[at], dst_ref=held.at[at],
                send_sem=a_send.at[part, step, mask - 1], recv_sem=a_recv.at[part, step, mask - 1],
                device_id=partner(stages[step], mask), device_id_type=MESH,
            )
            copy.start()
            out.append(copy)
        return out

    def factor_tiles(m, free, begin):
        @pl.loop(begin, 1 << len(free))
        def _(j):
            bits = []
            for link in held_links:
                own = bit_of(link)
                if link in free:
                    flip = lax.rem(lax.div(j, 1 << free.index(link)), 2)
                    own = own + flip * (1 - 2 * own)
                bits.append(own)
            start = 0
            for link, value in zip(held_links, bits):
                start = start + value * ((1 << link[1]) * (width if link[0] == "fsdp" else piece))
            here = pl.ds(pl.multiple_of(start, LANES), piece)
            high, low = split(held[tuple(bits) + (pl.ds(m * rank, rank), slice(None))])
            acc[m] += lax.dot_general(
                jnp.concatenate([high, low], axis=0), mhl[m, :, here], NT, preferred_element_type=F32
            )

    copies = [gather(part, 0) for part in range(2)]
    acc[...] = jnp.zeros_like(acc)
    for load in loads:
        load.wait()

    @pl.loop(0, cols // TILE)
    def _(t):
        here = pl.ds(pl.multiple_of(t * TILE, TILE), TILE)
        for m in range(2):
            high, low = split(g_buf[m, :, here].astype(F32) + e_buf[m, :, here])
            mhl[m, 0:rows, here] = high
            mhl[m, rows : 2 * rows, here] = low

    one, two, three = gather_parts[0][2]
    for step in range(3):
        for part in range(2):
            for copy in copies[part]:
                copy.wait()
            if step < 2:
                copies[part] = gather(part, step + 1)
        if step == 0:
            factor_tiles(0, one, 0)
        elif step == 1:
            factor_tiles(0, one + two, 1 << len(one))
            factor_tiles(1, one + two, 0)
        else:
            for m in range(2):
                factor_tiles(m, one + two + three, 1 << len(one + two))

    for m in range(2):
        whole = acc[m, 0:rank] + acc[m, rank : 2 * rank]
        one = whole[:, 0:rows] + whole[:, rows : 2 * rows]
        ft[0, m * rank : (m + 1) * rank] = jnp.concatenate([one, one], axis=1)
    for b in range(nr):
        copy = pltpu.make_async_remote_copy(
            src_ref=ft.at[b], dst_ref=ft_in.at[b], send_sem=f_send.at[b], recv_sem=f_recv.at[b],
            device_id=partner([("replica", b)], 1), device_id_type=MESH,
        )
        copy.start()
        copy.wait()
        ft[b + 1] = ft[b] + ft_in[b]
    factor = ft[nr] * (1.0 / replicas)
    f_high, f_low = split(factor)
    weights = [
        jnp.concatenate([f_high[m * rank : (m + 1) * rank], f_low[m * rank : (m + 1) * rank]], axis=0)
        for m in range(2)
    ]

    def term(m, start, count):
        @pl.loop(0, count // TILE)
        def _(t):
            here = pl.ds(pl.multiple_of(start + t * TILE, TILE), TILE)
            out = lax.dot_general(weights[m], mhl[m, :, here], NN, preferred_element_type=F32)
            z[m * rank : (m + 1) * rank, here] = out[0:rank] + out[rank : 2 * rank]

    half = cols // 2
    core = bit_of(("fsdp", 0))
    parts = range(len(reduce_parts))
    nsteps = 3
    shape = layout(nb, nr, cols)
    starts = [[0] for _ in parts]

    def send(p, step):
        low, high, stages = reduce_parts[p]
        cuts, sizes, offsets = shape[p]
        stage, size, start = stages[step], sizes[step + 1], starts[p][step]
        place = index_of(stage)
        starts[p].append(start + place * size if cuts[step] else start)
        if not cuts[step]:
            own_at = pl.multiple_of(offsets[step] + place * size, LANES)
            z_in[low:high, pl.ds(own_at, size)] = z[low:high, pl.ds(pl.multiple_of(start, LANES), size)]
        out = []
        for mask in masks(stage):
            if cuts[step]:
                away, land = start + index_of(stage, mask) * size, offsets[step] + (mask - 1) * size
            else:
                away, land = start, offsets[step] + place * size
            copy = pltpu.make_async_remote_copy(
                src_ref=z.at[pl.ds(low, high - low), pl.ds(pl.multiple_of(away, LANES), size)],
                dst_ref=z_in.at[pl.ds(low, high - low), pl.ds(pl.multiple_of(land, LANES), size)],
                send_sem=s_send.at[p, step, mask - 1], recv_sem=s_recv.at[p, step, mask - 1],
                device_id=partner(stage, mask), device_id_type=MESH,
            )
            copy.start()
            out.append(copy)
        return out

    def gram_send(step):
        stage = [link for link in reduce_parts[0][2][step] if link[0] == "fsdp"]
        place = index_of(stage)
        gram_in[step, place] = gram[step]
        out = []
        for mask in masks(stage):
            copy = pltpu.make_async_remote_copy(
                src_ref=gram.at[step], dst_ref=gram_in.at[step, place],
                send_sem=m_send.at[step, mask - 1], recv_sem=m_recv.at[step, mask - 1],
                device_id=partner(stage, mask), device_id_type=MESH,
            )
            copy.start()
            out.append(copy)
        return out

    copies = []
    for m in range(2):
        term(m, (1 - core) * half, half)
        copies += [send(p, 0) for p in parts if reduce_parts[p][0] // rank == m]
    product = lax.dot_general(
        factor, jnp.concatenate([factor, factor], axis=0), NT,
        precision=lax.Precision.HIGHEST, preferred_element_type=F32,
    ) * 0.5
    lane = lax.broadcasted_iota(jnp.int32, (rank, LANES), 1)
    gram[0] = jnp.where(lane < rank, product[0:rank], product[rank : 2 * rank])
    g_copies = gram_send(0)
    for m in range(2):
        term(m, core * half, half)
    for step in range(nsteps):
        for p in parts:
            low, high, stages = reduce_parts[p]
            cuts, sizes, offsets = shape[p]
            size = sizes[step + 1]
            for copy in copies[p]:
                copy.wait()
            here = pl.ds(pl.multiple_of(starts[p][step + 1], LANES), size)
            members = 1 << len(stages[step])
            terms = [
                z_in[low:high, offsets[step] + i * size : offsets[step] + (i + 1) * size]
                for i in range(members - cuts[step])
            ]
            added = z[low:high, here] + terms[0] if cuts[step] else terms[0]
            for term_in in terms[1:]:
                added = added + term_in
            if step + 1 < nsteps:
                z[low:high, here] = added
                copies[p] = send(p, step + 1)
            else:
                total[low:high, here] = added
        for copy in g_copies:
            copy.wait()
        members = len(g_copies) + 1
        summed = gram_in[step, 0]
        for i in range(1, members):
            summed = summed + gram_in[step, i]
        gram[step + 1] = summed
        g_copies = gram_send(step + 1) if step + 1 < nsteps else []

    def back(p, step):
        low, high, stages = reduce_parts[p]
        cuts, sizes, _ = shape[p]
        if not cuts[step]:
            return []
        at = (pl.ds(low, high - low), pl.ds(pl.multiple_of(starts[p][step + 1], LANES), sizes[step + 1]))
        out = []
        for mask in masks(stages[step]):
            copy = pltpu.make_async_remote_copy(
                src_ref=total.at[at], dst_ref=total.at[at],
                send_sem=b_send.at[p, step, mask - 1], recv_sem=b_recv.at[p, step, mask - 1],
                device_id=partner(stages[step], mask), device_id_type=MESH,
            )
            copy.start()
            out.append(copy)
        return out

    def advance(step):
        for p in parts:
            for copy in copies[p]:
                copy.wait()
            copies[p] = back(p, step - 1) if step > 0 else []

    copies = [back(p, nsteps - 1) for p in parts]

    row = lax.broadcasted_iota(jnp.int32, (rank, LANES), 0)
    lane = lax.broadcasted_iota(jnp.int32, (rank, LANES), 1)
    first = lax.rem(lane, 2 * rank) < rank
    work = jnp.where(lane < 2 * rank, gram[nsteps], jnp.where(lax.rem(lane, rank) == row, 1.0, 0.0))
    for j in range(rank):
        if j == 12:
            advance(2)
        column = jnp.where(first, work[:, j : j + 1], work[:, rank + j : rank + j + 1])
        top = work[j : j + 1, :] / column[j : j + 1, :]
        work = jnp.where(row > j, work - column * top, work)
    pivots = [
        jnp.sum(jnp.where(lane == row + m * rank, work, 0.0), axis=1, keepdims=True) for m in range(2)
    ]
    scaled = work / jnp.sqrt(jnp.where(first, pivots[0], pivots[1]))
    inv = [scaled[:, (2 + m) * rank : (3 + m) * rank] for m in range(2)]
    for m in range(2):
        solved = lax.dot_general(
            inv[m], factor[m * rank : (m + 1) * rank, 0:rows], NN,
            precision=lax.Precision.HIGHEST, preferred_element_type=F32,
        )
        left_t[m * rank : (m + 1) * rank] = solved
        folded[m] = lax.dot_general(
            solved, inv[m], TN, precision=lax.Precision.HIGHEST, preferred_element_type=F32
        ) * (1.0 / replicas)

    advance(1)
    advance(0)
    own = pl.ds(pl.multiple_of(f * width, LANES), width)
    for m in range(2):
        at = slice(m * rank, (m + 1) * rank)
        own_basis[at] = dot32(inv[m], total[at, own], NN) * (1.0 / replicas)


def finish(grads, errors, total, folded, left_in, basis_in, out, left_out, basis_out):
    rank = total.shape[0] // 2

    @pl.when(pl.program_id(0) == 0)
    def _():
        left_out[...] = left_in[...]
        basis_out[...] = basis_in[...]

    for m in range(2):
        approx = dot32(folded[m], total[m * rank : (m + 1) * rank], NN)
        out[m] = grads[m].astype(F32) + errors[m] - approx


def solution(mesh):
    n, replicas = mesh.shape["fsdp"], mesh.shape["replica"]
    nb, nr = log2(n), log2(replicas)

    def shards(grads, errors, basis):
        _, nmat, rows, cols = grads.shape
        width, _, rank = basis.shape
        grads, errors = grads[0], errors[0]
        basis_t = jnp.transpose(basis, (1, 2, 0)).reshape(nmat * rank, width)
        full = nmat * rank
        share = width // replicas >= LANES
        piece = width // replicas if share else width
        reduce_parts = plan(nb, nr, share)[0]
        nparts, steps = len(reduce_parts), 3
        most = max(1 << len(stage) for stage in reduce_parts[0][2])
        arrivals = max(offsets[-1] for _, _, offsets in layout(nb, nr, cols))
        vmem = pl.BlockSpec(memory_space=pltpu.VMEM)
        hbm = pl.BlockSpec(memory_space=pl.ANY)
        dma = pltpu.SemaphoreType.DMA
        total, left_t, own_basis, folded = pl.pallas_call(
            functools.partial(exchange, n, replicas, share),
            out_shape=[
                jax.ShapeDtypeStruct((full, cols), F32),
                jax.ShapeDtypeStruct((full, rows), F32),
                jax.ShapeDtypeStruct((full, width), F32),
                jax.ShapeDtypeStruct((nmat, rows, rank), F32),
            ],
            in_specs=[hbm, hbm, vmem],
            out_specs=[vmem] * 4,
            scratch_shapes=[
                pltpu.VMEM((2,) * (nb + nr * share) + (full, piece), F32),
                pltpu.VMEM((nmat, rows, cols), BF16),
                pltpu.VMEM((nmat, rows, cols), F32),
                pltpu.VMEM((nmat, 2 * rows, cols), BF16),
                pltpu.VMEM((nmat, 2 * rank, 2 * rows), F32),
                pltpu.VMEM((nr + 1, full, 2 * rows), F32),
                pltpu.VMEM((nr, full, 2 * rows), F32),
                pltpu.VMEM((full, cols), F32),
                pltpu.VMEM((full, arrivals), F32),
                pltpu.VMEM((steps + 1, rank, LANES), F32),
                pltpu.VMEM((steps, most, rank, LANES), F32),
                dma((2,)),
                dma((2, 3, most)), dma((2, 3, most)),
                dma((nr,)), dma((nr,)),
                dma((nparts, steps, most)), dma((nparts, steps, most)),
                dma((steps, most)), dma((steps, most)),
                dma((nparts, steps, most)), dma((nparts, steps, most)),
            ],
            compiler_params=pltpu.CompilerParams(
                collective_id=0, has_side_effects=True, vmem_limit_bytes=60 * 1024 * 1024
            ),
        )(grads, errors, basis_t)

        block = 1024
        whole = lambda a: pl.BlockSpec(a.shape, lambda i: (0,) * a.ndim)
        new_errors, left_t, own_basis = pl.pallas_call(
            finish,
            grid=(cols // block,),
            out_shape=[
                jax.ShapeDtypeStruct((nmat, rows, cols), F32),
                jax.ShapeDtypeStruct(left_t.shape, F32),
                jax.ShapeDtypeStruct(own_basis.shape, F32),
            ],
            in_specs=[
                pl.BlockSpec((nmat, rows, block), lambda i: (0, 0, i)),
                pl.BlockSpec((nmat, rows, block), lambda i: (0, 0, i)),
                pl.BlockSpec((full, block), lambda i: (0, i)),
                whole(folded),
                whole(left_t),
                whole(own_basis),
            ],
            out_specs=[
                pl.BlockSpec((nmat, rows, block), lambda i: (0, 0, i)),
                whole(left_t),
                whole(own_basis),
            ],
            compiler_params=pltpu.CompilerParams(vmem_limit_bytes=60 * 1024 * 1024),
        )(grads, errors, total, folded, left_t, own_basis)
        left = jnp.transpose(left_t.reshape(nmat, rank, rows), (0, 2, 1))
        new_basis = jnp.transpose(own_basis.reshape(nmat, rank, width), (2, 0, 1))
        return (new_errors[None], left, new_basis)

    in_specs = (
        P("replica", None, "fsdp", None),
        P("replica", None, "fsdp", None),
        P("fsdp", None, None),
    )
    out_specs = (P("replica", None, "fsdp", None), P(None, "fsdp", None), P("fsdp", None, None))
    return jax.shard_map(shards, mesh=mesh, in_specs=in_specs, out_specs=out_specs, check_vma=False)
```

```python
import functools

import jax
import jax.numpy as jnp
from jax import lax
from jax.experimental import pallas as pl
from jax.experimental.pallas import tpu as pltpu
from jax.sharding import PartitionSpec as P

MESH = pl.DeviceIdType.MESH
F32, BF16 = jnp.float32, jnp.bfloat16
TILE = 512
LANES = 128
NT = (((1,), (1,)), ((), ()))
NN = (((1,), (0,)), ((), ()))
TN = (((0,), (0,)), ((), ()))


def split(x):
    high = x.astype(BF16)
    return high, (x - high.astype(F32)).astype(BF16)


def dot32(a, b, dims):
    (ca,), (cb,) = dims[0]
    ah, al = split(a)
    bh, bl = split(b)
    left = jnp.concatenate([ah, ah, al], axis=ca)
    right = jnp.concatenate([bh, bl, bh], axis=cb)
    return lax.dot_general(left, right, dims, preferred_element_type=F32)


def log2(n):
    return n.bit_length() - 1


def plan(nb, nr, share):
    core, near = [("fsdp", 0)], [("fsdp", 1)]
    far = [("fsdp", b) for b in range(2, nb)]
    across = [("replica", b) for b in range(nr)]
    plane_first = [core, near + across, far]
    far_first = [core, far, near + across]
    reduce_parts = [
        (0, 16, plane_first), (16, 32, plane_first), (32, 40, plane_first),
        (40, 48, far_first), (48, 64, far_first),
    ]
    plane = near + across if share else near
    gather_parts = [(0, 40, [far, plane, core]), (40, 64, [plane, far, core])]
    return reduce_parts, gather_parts


def layout(nb, nr, cols):
    out = []
    for _, _, stages in plan(nb, nr, False)[0]:
        cuts, sizes, offsets = [], [cols], [0]
        for stage in stages:
            members = 1 << len(stage)
            cuts.append(sizes[-1] // members >= LANES)
            sizes.append(sizes[-1] // members if cuts[-1] else sizes[-1])
            offsets.append(offsets[-1] + (members - cuts[-1]) * sizes[-1])
        out.append((cuts, sizes, offsets))
    return out


def exchange(
    n, replicas, share, grads, errors, basis, merged, total, left_t, own_basis, folded,
    held, g_buf, mhl, acc, ft, ft_in, z, z_in, gram, gram_in,
    load_sem, a_send, a_recv, f_send, f_recv, s_send, s_recv, m_send, m_recv, b_send, b_recv,
):
    nb, nr = log2(n), log2(replicas)
    reduce_parts, gather_parts = plan(nb, nr, share)
    rank = basis.shape[0] // 2
    width = basis.shape[1]
    rows = grads.shape[1]
    cols = grads.shape[2]
    y, f = lax.axis_index("replica"), lax.axis_index("fsdp")

    def bit_of(link):
        return lax.rem(lax.div(f if link[0] == "fsdp" else y, 1 << link[1]), 2)

    def index_of(stage, mask=0):
        total_index = 0
        for i, link in enumerate(stage):
            own = bit_of(link)
            total_index = total_index + (1 - own if mask >> i & 1 else own) * (1 << i)
        return total_index

    def partner(stage, mask):
        there = {"replica": y, "fsdp": f}
        for i, link in enumerate(stage):
            if mask >> i & 1:
                there[link[0]] = there[link[0]] + (1 - 2 * bit_of(link)) * (1 << link[1])
        return (there["replica"], there["fsdp"])

    def masks(stage):
        return range(1, 1 << len(stage))

    loads = [
        pltpu.make_async_copy(grads, g_buf, load_sem.at[0]),
        pltpu.make_async_copy(errors, merged, load_sem.at[1]),
    ]
    for load in loads:
        load.start()

    barrier = pltpu.get_barrier_semaphore()
    peers = [(stage, mask) for stage in reduce_parts[0][2] for mask in masks(stage)]
    for stage, mask in peers:
        pl.semaphore_signal(barrier, inc=1, device_id=partner(stage, mask), device_id_type=MESH)
    held_links = [("fsdp", b) for b in range(nb - 1, -1, -1)]
    if share:
        held_links += [("replica", b) for b in range(nr - 1, -1, -1)]
    piece = held.shape[-1]
    mine = tuple(bit_of(link) for link in held_links)
    first_column = sum(bit_of(link) * (1 << link[1]) for link in held_links if link[0] == "replica") * piece
    if share:
        held[mine] = basis[:, pl.ds(pl.multiple_of(first_column, LANES), piece)]
    else:
        held[mine] = basis[...]
    pl.semaphore_wait(barrier, len(peers))

    def gather(part, step):
        low, high, stages = gather_parts[part]
        done = [link for stage in stages[:step] for link in stage]
        at = tuple(slice(None) if link in done else bit_of(link) for link in held_links)
        at = at + (pl.ds(low, high - low), slice(None))
        out = []
        for mask in masks(stages[step]):
            copy = pltpu.make_async_remote_copy(
                src_ref=held.at[at], dst_ref=held.at[at],
                send_sem=a_send.at[part, step, mask - 1], recv_sem=a_recv.at[part, step, mask - 1],
                device_id=partner(stages[step], mask), device_id_type=MESH,
            )
            copy.start()
            out.append(copy)
        return out

    def factor_tiles(m, free, begin):
        end = 1 << len(free)
        group = 8 if begin % 8 == 0 and end % 8 == 0 else 4

        @pl.loop(begin // group, end // group)
        def _(outer):
            summed = 0.0
            for inner in range(group):
                j = outer * group + inner
                bits = []
                for link in held_links:
                    own = bit_of(link)
                    if link in free:
                        flip = lax.rem(lax.div(j, 1 << free.index(link)), 2)
                        own = own + flip * (1 - 2 * own)
                    bits.append(own)
                start = 0
                for link, value in zip(held_links, bits):
                    start = start + value * ((1 << link[1]) * (width if link[0] == "fsdp" else piece))
                here = pl.ds(pl.multiple_of(start, LANES), piece)
                high, low = split(held[tuple(bits) + (pl.ds(m * rank, rank), slice(None))])
                summed = summed + lax.dot_general(
                    jnp.concatenate([high, low], axis=0), mhl[m, :, here], NT, preferred_element_type=F32
                )
            acc[m] += summed

    copies = [gather(part, 0) for part in range(2)]
    acc[...] = jnp.zeros_like(acc)
    for load in loads:
        load.wait()

    @pl.loop(0, cols // TILE)
    def _(t):
        here = pl.ds(pl.multiple_of(t * TILE, TILE), TILE)
        for m in range(2):
            both = g_buf[m, :, here].astype(F32) + merged[m, :, here]
            merged[m, :, here] = both
            high, low = split(both)
            mhl[m, 0:rows, here] = high
            mhl[m, rows : 2 * rows, here] = low

    one, two, three = gather_parts[0][2]
    for step in range(3):
        for part in range(2):
            for copy in copies[part]:
                copy.wait()
            if step < 2:
                copies[part] = gather(part, step + 1)
        if step == 0:
            factor_tiles(0, one, 0)
        elif step == 1:
            factor_tiles(0, one + two, 1 << len(one))
            factor_tiles(1, one + two, 0)
        else:
            for m in range(2):
                factor_tiles(m, one + two + three, 1 << len(one + two))

    for m in range(2):
        whole = acc[m, 0:rank] + acc[m, rank : 2 * rank]
        one = whole[:, 0:rows] + whole[:, rows : 2 * rows]
        ft[0, m * rank : (m + 1) * rank] = jnp.concatenate([one, one], axis=1)
    for b in range(nr):
        copy = pltpu.make_async_remote_copy(
            src_ref=ft.at[b], dst_ref=ft_in.at[b], send_sem=f_send.at[b], recv_sem=f_recv.at[b],
            device_id=partner([("replica", b)], 1), device_id_type=MESH,
        )
        copy.start()
        copy.wait()
        ft[b + 1] = ft[b] + ft_in[b]
    factor = ft[nr] * (1.0 / replicas)
    f_high, f_low = split(factor)
    weights = [
        jnp.concatenate([f_high[m * rank : (m + 1) * rank], f_low[m * rank : (m + 1) * rank]], axis=0)
        for m in range(2)
    ]

    def term(m, start, count):
        @pl.loop(0, count // (2 * TILE))
        def _(t):
            here = pl.ds(pl.multiple_of(start + t * 2 * TILE, 2 * TILE), 2 * TILE)
            out = lax.dot_general(weights[m], mhl[m, :, here], NN, preferred_element_type=F32)
            z[m * rank : (m + 1) * rank, here] = out[0:rank] + out[rank : 2 * rank]

    half = cols // 2
    core = bit_of(("fsdp", 0))
    parts = range(len(reduce_parts))
    nsteps = 3
    shape = layout(nb, nr, cols)
    starts = [[0] for _ in parts]

    def send(p, step):
        low, high, stages = reduce_parts[p]
        cuts, sizes, offsets = shape[p]
        stage, size, start = stages[step], sizes[step + 1], starts[p][step]
        place = index_of(stage)
        starts[p].append(start + place * size if cuts[step] else start)
        if not cuts[step]:
            own_at = pl.multiple_of(offsets[step] + place * size, LANES)
            z_in[low:high, pl.ds(own_at, size)] = z[low:high, pl.ds(pl.multiple_of(start, LANES), size)]
        out = []
        for mask in masks(stage):
            if cuts[step]:
                away, land = start + index_of(stage, mask) * size, offsets[step] + (mask - 1) * size
            else:
                away, land = start, offsets[step] + place * size
            copy = pltpu.make_async_remote_copy(
                src_ref=z.at[pl.ds(low, high - low), pl.ds(pl.multiple_of(away, LANES), size)],
                dst_ref=z_in.at[pl.ds(low, high - low), pl.ds(pl.multiple_of(land, LANES), size)],
                send_sem=s_send.at[p, step, mask - 1], recv_sem=s_recv.at[p, step, mask - 1],
                device_id=partner(stage, mask), device_id_type=MESH,
            )
            copy.start()
            out.append(copy)
        return out

    def gram_send(step):
        stage = [link for link in reduce_parts[0][2][step] if link[0] == "fsdp"]
        place = index_of(stage)
        gram_in[step, place] = gram[step]
        out = []
        for mask in masks(stage):
            copy = pltpu.make_async_remote_copy(
                src_ref=gram.at[step], dst_ref=gram_in.at[step, place],
                send_sem=m_send.at[step, mask - 1], recv_sem=m_recv.at[step, mask - 1],
                device_id=partner(stage, mask), device_id_type=MESH,
            )
            copy.start()
            out.append(copy)
        return out

    copies = []
    for m in range(2):
        term(m, (1 - core) * half, half)
        copies += [send(p, 0) for p in parts if reduce_parts[p][0] // rank == m]
    product = lax.dot_general(
        factor, jnp.concatenate([factor, factor], axis=0), NT,
        precision=lax.Precision.HIGHEST, preferred_element_type=F32,
    ) * 0.5
    lane = lax.broadcasted_iota(jnp.int32, (rank, LANES), 1)
    gram[0] = jnp.where(lane < rank, product[0:rank], product[rank : 2 * rank])
    g_copies = gram_send(0)
    for m in range(2):
        term(m, core * half, half)
    for step in range(nsteps):
        for p in parts:
            low, high, stages = reduce_parts[p]
            cuts, sizes, offsets = shape[p]
            size = sizes[step + 1]
            for copy in copies[p]:
                copy.wait()
            here = pl.ds(pl.multiple_of(starts[p][step + 1], LANES), size)
            members = 1 << len(stages[step])
            terms = [
                z_in[low:high, offsets[step] + i * size : offsets[step] + (i + 1) * size]
                for i in range(members - cuts[step])
            ]
            added = z[low:high, here] + terms[0] if cuts[step] else terms[0]
            for term_in in terms[1:]:
                added = added + term_in
            if step + 1 < nsteps:
                z[low:high, here] = added
                copies[p] = send(p, step + 1)
            else:
                total[low:high, here] = added
        for copy in g_copies:
            copy.wait()
        members = len(g_copies) + 1
        summed = gram_in[step, 0]
        for i in range(1, members):
            summed = summed + gram_in[step, i]
        gram[step + 1] = summed
        g_copies = gram_send(step + 1) if step + 1 < nsteps else []

    def back(p, step):
        low, high, stages = reduce_parts[p]
        cuts, sizes, _ = shape[p]
        if not cuts[step]:
            return []
        at = (pl.ds(low, high - low), pl.ds(pl.multiple_of(starts[p][step + 1], LANES), sizes[step + 1]))
        out = []
        for mask in masks(stages[step]):
            copy = pltpu.make_async_remote_copy(
                src_ref=total.at[at], dst_ref=total.at[at],
                send_sem=b_send.at[p, step, mask - 1], recv_sem=b_recv.at[p, step, mask - 1],
                device_id=partner(stages[step], mask), device_id_type=MESH,
            )
            copy.start()
            out.append(copy)
        return out

    def advance(step):
        for p in parts:
            for copy in copies[p]:
                copy.wait()
            copies[p] = back(p, step - 1) if step > 0 else []

    copies = [back(p, nsteps - 1) for p in parts]

    row = lax.broadcasted_iota(jnp.int32, (rank, LANES), 0)
    lane = lax.broadcasted_iota(jnp.int32, (rank, LANES), 1)
    first = lax.rem(lane, 2 * rank) < rank
    work = jnp.where(lane < 2 * rank, gram[nsteps], jnp.where(lax.rem(lane, rank) == row, 1.0, 0.0))
    for j in range(rank):
        if j == 12:
            advance(2)
        column = jnp.where(first, work[:, j : j + 1], work[:, rank + j : rank + j + 1])
        top = work[j : j + 1, :] / column[j : j + 1, :]
        work = jnp.where(row > j, work - column * top, work)
    pivots = [
        jnp.sum(jnp.where(lane == row + m * rank, work, 0.0), axis=1, keepdims=True) for m in range(2)
    ]
    scaled = work / jnp.sqrt(jnp.where(first, pivots[0], pivots[1]))
    inv = [scaled[:, (2 + m) * rank : (3 + m) * rank] for m in range(2)]
    for m in range(2):
        solved = lax.dot_general(
            inv[m], factor[m * rank : (m + 1) * rank, 0:rows], NN,
            precision=lax.Precision.HIGHEST, preferred_element_type=F32,
        )
        left_t[m * rank : (m + 1) * rank] = solved
        folded[m] = lax.dot_general(
            solved, inv[m], TN, precision=lax.Precision.HIGHEST, preferred_element_type=F32
        ) * (1.0 / replicas)

    advance(1)
    advance(0)
    own = pl.ds(pl.multiple_of(f * width, LANES), width)
    for m in range(2):
        at = slice(m * rank, (m + 1) * rank)
        own_basis[at] = dot32(inv[m], total[at, own], NN) * (1.0 / replicas)


def finish(merged, total, folded, left_in, basis_in, out, left_out, basis_out):
    rank = total.shape[0] // 2
    block = out.shape[2]
    here = pl.ds(pl.multiple_of(pl.program_id(0) * block, block), block)

    @pl.when(pl.program_id(0) == 0)
    def _():
        left_out[...] = left_in[...]
        basis_out[...] = basis_in[...]

    for m in range(2):
        approx = dot32(folded[m], total[m * rank : (m + 1) * rank, here], NN)
        out[m] = merged[m, :, here] - approx


def solution(mesh):
    n, replicas = mesh.shape["fsdp"], mesh.shape["replica"]
    nb, nr = log2(n), log2(replicas)

    def shards(grads, errors, basis):
        _, nmat, rows, cols = grads.shape
        width, _, rank = basis.shape
        grads, errors = grads[0], errors[0]
        basis_t = jnp.transpose(basis, (1, 2, 0)).reshape(nmat * rank, width)
        full = nmat * rank
        share = width // replicas >= LANES
        piece = width // replicas if share else width
        reduce_parts = plan(nb, nr, share)[0]
        nparts, steps = len(reduce_parts), 3
        most = max(1 << len(stage) for stage in reduce_parts[0][2])
        arrivals = max(offsets[-1] for _, _, offsets in layout(nb, nr, cols))
        vmem = pl.BlockSpec(memory_space=pltpu.VMEM)
        hbm = pl.BlockSpec(memory_space=pltpu.HBM)
        dma = pltpu.SemaphoreType.DMA
        merged, total, left_t, own_basis, folded = pl.pallas_call(
            functools.partial(exchange, n, replicas, share),
            out_shape=[
                pltpu.VMEM((nmat, rows, cols), F32),
                pltpu.VMEM((full, cols), F32),
                pltpu.VMEM((full, rows), F32),
                pltpu.VMEM((full, width), F32),
                pltpu.VMEM((nmat, rows, rank), F32),
            ],
            in_specs=[hbm, hbm, vmem],
            out_specs=[vmem] * 5,
            scratch_shapes=[
                pltpu.VMEM((2,) * (nb + nr * share) + (full, piece), F32),
                pltpu.VMEM((nmat, rows, cols), BF16),
                pltpu.VMEM((nmat, 2 * rows, cols), BF16),
                pltpu.VMEM((nmat, 2 * rank, 2 * rows), F32),
                pltpu.VMEM((nr + 1, full, 2 * rows), F32),
                pltpu.VMEM((nr, full, 2 * rows), F32),
                pltpu.VMEM((full, cols), F32),
                pltpu.VMEM((full, arrivals), F32),
                pltpu.VMEM((steps + 1, rank, LANES), F32),
                pltpu.VMEM((steps, most, rank, LANES), F32),
                dma((2,)),
                dma((2, 3, most)), dma((2, 3, most)),
                dma((nr,)), dma((nr,)),
                dma((nparts, steps, most)), dma((nparts, steps, most)),
                dma((steps, most)), dma((steps, most)),
                dma((nparts, steps, most)), dma((nparts, steps, most)),
            ],
            compiler_params=pltpu.CompilerParams(
                collective_id=0, has_side_effects=True, vmem_limit_bytes=56 * 1024 * 1024
            ),
        )(grads, errors, basis_t)

        block = 1024
        whole = lambda a: pl.BlockSpec(a.shape, lambda i: (0,) * a.ndim)
        new_errors, left_t, own_basis = pl.pallas_call(
            finish,
            grid=(cols // block,),
            out_shape=[
                jax.ShapeDtypeStruct((nmat, rows, cols), F32),
                jax.ShapeDtypeStruct(left_t.shape, F32),
                jax.ShapeDtypeStruct(own_basis.shape, F32),
            ],
            in_specs=[
                vmem,
                vmem,
                vmem,
                vmem,
                vmem,
            ],
            out_specs=[
                pl.BlockSpec((nmat, rows, block), lambda i: (0, 0, i)),
                whole(left_t),
                whole(own_basis),
            ],
            compiler_params=pltpu.CompilerParams(vmem_limit_bytes=24 * 1024 * 1024),
        )(merged, total, folded, left_t, own_basis)
        left = jnp.transpose(left_t.reshape(nmat, rank, rows), (0, 2, 1))
        new_basis = jnp.transpose(own_basis.reshape(nmat, rank, width), (2, 0, 1))
        return (new_errors[None], left, new_basis)

    in_specs = (
        P("replica", None, "fsdp", None),
        P("replica", None, "fsdp", None),
        P("fsdp", None, None),
    )
    out_specs = (P("replica", None, "fsdp", None), P(None, "fsdp", None), P("fsdp", None, None))
    return jax.shard_map(shards, mesh=mesh, in_specs=in_specs, out_specs=out_specs, check_vma=False)
```

```python
import functools

import jax
import jax.numpy as jnp
from jax import lax
from jax.experimental import pallas as pl
from jax.experimental.pallas import tpu as pltpu
from jax.sharding import PartitionSpec as P

MESH = pl.DeviceIdType.MESH
F32, BF16 = jnp.float32, jnp.bfloat16
TILE = 512
LANES = 128
NT = (((1,), (1,)), ((), ()))
NN = (((1,), (0,)), ((), ()))
TN = (((0,), (0,)), ((), ()))


def split(x):
    high = x.astype(BF16)
    return high, (x - high.astype(F32)).astype(BF16)


def dot32(a, b, dims):
    (ca,), (cb,) = dims[0]
    ah, al = split(a)
    bh, bl = split(b)
    left = jnp.concatenate([ah, ah, al], axis=ca)
    right = jnp.concatenate([bh, bl, bh], axis=cb)
    return lax.dot_general(left, right, dims, preferred_element_type=F32)


def log2(n):
    return n.bit_length() - 1


def plan(nb, nr, share):
    core, near = [("fsdp", 0)], [("fsdp", 1)]
    far = [("fsdp", b) for b in range(2, nb)]
    across = [("replica", b) for b in range(nr)]
    plane_first = [core, near + across, far]
    far_first = [core, far, near + across]
    reduce_parts = [
        (0, 16, plane_first), (16, 32, plane_first), (32, 40, plane_first),
        (40, 48, far_first), (48, 64, far_first),
    ]
    plane = near + across if share else near
    gather_parts = [(0, 40, [far, plane, core]), (40, 64, [plane, far, core])]
    return reduce_parts, gather_parts


def layout(nb, nr, cols):
    out = []
    for _, _, stages in plan(nb, nr, False)[0]:
        cuts, sizes, offsets = [], [cols], [0]
        for stage in stages:
            members = 1 << len(stage)
            cuts.append(sizes[-1] // members >= LANES)
            sizes.append(sizes[-1] // members if cuts[-1] else sizes[-1])
            offsets.append(offsets[-1] + (members - cuts[-1]) * sizes[-1])
        out.append((cuts, sizes, offsets))
    return out


def exchange(
    n, replicas, share, grads, errors, basis, merged, total, left_t, own_basis, folded,
    held, g_buf, mhl, acc, ft, ft_in, z, z_in, gram, gram_in,
    load_sem, a_send, a_recv, f_send, f_recv, s_send, s_recv, m_send, m_recv, b_send, b_recv,
):
    nb, nr = log2(n), log2(replicas)
    reduce_parts, gather_parts = plan(nb, nr, share)
    rank = basis.shape[0] // 2
    width = basis.shape[1]
    rows = grads.shape[1]
    cols = grads.shape[2]
    y, f = lax.axis_index("replica"), lax.axis_index("fsdp")

    def bit_of(link):
        return lax.rem(lax.div(f if link[0] == "fsdp" else y, 1 << link[1]), 2)

    def index_of(stage, mask=0):
        total_index = 0
        for i, link in enumerate(stage):
            own = bit_of(link)
            total_index = total_index + (1 - own if mask >> i & 1 else own) * (1 << i)
        return total_index

    def partner(stage, mask):
        there = {"replica": y, "fsdp": f}
        for i, link in enumerate(stage):
            if mask >> i & 1:
                there[link[0]] = there[link[0]] + (1 - 2 * bit_of(link)) * (1 << link[1])
        return (there["replica"], there["fsdp"])

    def masks(stage):
        return range(1, 1 << len(stage))

    loads = [
        [
            pltpu.make_async_copy(grads.at[m], g_buf.at[m], load_sem.at[m, 0]),
            pltpu.make_async_copy(errors.at[m], merged.at[m], load_sem.at[m, 1]),
        ]
        for m in range(2)
    ]
    for load in loads[0] + loads[1]:
        load.start()

    barrier = pltpu.get_barrier_semaphore()
    peers = [(stage, mask) for stage in reduce_parts[0][2] for mask in masks(stage)]
    for stage, mask in peers:
        pl.semaphore_signal(barrier, inc=1, device_id=partner(stage, mask), device_id_type=MESH)
    held_links = [("fsdp", b) for b in range(nb - 1, -1, -1)]
    if share:
        held_links += [("replica", b) for b in range(nr - 1, -1, -1)]
    piece = held.shape[-1]
    mine = tuple(bit_of(link) for link in held_links)
    first_column = sum(bit_of(link) * (1 << link[1]) for link in held_links if link[0] == "replica") * piece
    if share:
        held[mine] = basis[:, pl.ds(pl.multiple_of(first_column, LANES), piece)]
    else:
        held[mine] = basis[...]
    pl.semaphore_wait(barrier, len(peers))

    def gather(part, step):
        low, high, stages = gather_parts[part]
        done = [link for stage in stages[:step] for link in stage]
        at = tuple(slice(None) if link in done else bit_of(link) for link in held_links)
        at = at + (pl.ds(low, high - low), slice(None))
        out = []
        for mask in masks(stages[step]):
            copy = pltpu.make_async_remote_copy(
                src_ref=held.at[at], dst_ref=held.at[at],
                send_sem=a_send.at[part, step, mask - 1], recv_sem=a_recv.at[part, step, mask - 1],
                device_id=partner(stages[step], mask), device_id_type=MESH,
            )
            copy.start()
            out.append(copy)
        return out

    def factor_tiles(m, free, begin):
        end = 1 << len(free)
        group = 8 if begin % 8 == 0 and end % 8 == 0 else 4

        @pl.loop(begin // group, end // group)
        def _(outer):
            summed = 0.0
            for inner in range(group):
                j = outer * group + inner
                bits = []
                for link in held_links:
                    own = bit_of(link)
                    if link in free:
                        flip = lax.rem(lax.div(j, 1 << free.index(link)), 2)
                        own = own + flip * (1 - 2 * own)
                    bits.append(own)
                start = 0
                for link, value in zip(held_links, bits):
                    start = start + value * ((1 << link[1]) * (width if link[0] == "fsdp" else piece))
                here = pl.ds(pl.multiple_of(start, LANES), piece)
                high, low = split(held[tuple(bits) + (pl.ds(m * rank, rank), slice(None))])
                summed = summed + lax.dot_general(
                    jnp.concatenate([high, low], axis=0), mhl[m, :, here], NT, preferred_element_type=F32
                )
            acc[m] += summed

    copies = [gather(part, 0) for part in range(2)]
    acc[...] = jnp.zeros_like(acc)

    def convert(m):
        for load in loads[m]:
            load.wait()

        @pl.loop(0, cols // (2 * TILE))
        def _(t):
            here = pl.ds(pl.multiple_of(t * 2 * TILE, 2 * TILE), 2 * TILE)
            both = g_buf[m, :, here].astype(F32) + merged[m, :, here]
            merged[m, :, here] = both
            high, low = split(both)
            mhl[m, 0:rows, here] = high
            mhl[m, rows : 2 * rows, here] = low

    one, two, three = gather_parts[0][2]

    def arrive(part, step):
        for copy in copies[part]:
            copy.wait()
        copies[part] = gather(part, step + 1) if step < 2 else []

    def factor_send(m, b):
        copy = pltpu.make_async_remote_copy(
            src_ref=ft.at[b, m], dst_ref=ft_in.at[b, m],
            send_sem=f_send.at[b, m], recv_sem=f_recv.at[b, m],
            device_id=partner([("replica", b)], 1), device_id_type=MESH,
        )
        copy.start()
        return copy

    def factor_first(m):
        factor_tiles(m, one + two + three, 1 << len(one + two))
        whole = acc[m, 0:rank] + acc[m, rank : 2 * rank]
        single = whole[:, 0:rows] + whole[:, rows : 2 * rows]
        ft[0, m] = jnp.concatenate([single, single], axis=1)
        return factor_send(m, 0)

    def factor_last(m, copy):
        for b in range(nr):
            copy.wait()
            ft[b + 1, m] = ft[b, m] + ft_in[b, m]
            if b + 1 < nr:
                copy = factor_send(m, b + 1)
        return ft[nr, m] * (1.0 / replicas)

    convert(0)
    for part in range(2):
        arrive(part, 0)
    convert(1)
    factor_tiles(0, one, 0)
    for part in range(2):
        arrive(part, 1)
    factor_tiles(0, one + two, 1 << len(one))
    factor_tiles(1, one + two, 0)
    arrive(0, 2)
    f_copies = [factor_first(0)]
    arrive(1, 2)
    f_copies.append(factor_first(1))

    def term(m, start, count):
        high, low = split(factors[m])
        weights = jnp.concatenate([high, low], axis=0)

        @pl.loop(0, count // (4 * TILE))
        def _(t):
            here = pl.ds(pl.multiple_of(start + t * 4 * TILE, 4 * TILE), 4 * TILE)
            out = lax.dot_general(weights, mhl[m, :, here], NN, preferred_element_type=F32)
            z[m * rank : (m + 1) * rank, here] = out[0:rank] + out[rank : 2 * rank]

    half = cols // 2
    core = bit_of(("fsdp", 0))
    parts = range(len(reduce_parts))
    nsteps = 3
    shape = layout(nb, nr, cols)
    starts = [[0] for _ in parts]

    def send(p, step):
        low, high, stages = reduce_parts[p]
        cuts, sizes, offsets = shape[p]
        stage, size, start = stages[step], sizes[step + 1], starts[p][step]
        place = index_of(stage)
        starts[p].append(start + place * size if cuts[step] else start)
        if not cuts[step]:
            own_at = pl.multiple_of(offsets[step] + place * size, LANES)
            z_in[low:high, pl.ds(own_at, size)] = z[low:high, pl.ds(pl.multiple_of(start, LANES), size)]
        out = []
        for mask in masks(stage):
            if cuts[step]:
                away, land = start + index_of(stage, mask) * size, offsets[step] + (mask - 1) * size
            else:
                away, land = start, offsets[step] + place * size
            copy = pltpu.make_async_remote_copy(
                src_ref=z.at[pl.ds(low, high - low), pl.ds(pl.multiple_of(away, LANES), size)],
                dst_ref=z_in.at[pl.ds(low, high - low), pl.ds(pl.multiple_of(land, LANES), size)],
                send_sem=s_send.at[p, step, mask - 1], recv_sem=s_recv.at[p, step, mask - 1],
                device_id=partner(stage, mask), device_id_type=MESH,
            )
            copy.start()
            out.append(copy)
        return out

    def gram_send(step):
        stage = [link for link in reduce_parts[0][2][step] if link[0] == "fsdp"]
        place = index_of(stage)
        gram_in[step, place] = gram[step]
        out = []
        for mask in masks(stage):
            copy = pltpu.make_async_remote_copy(
                src_ref=gram.at[step], dst_ref=gram_in.at[step, place],
                send_sem=m_send.at[step, mask - 1], recv_sem=m_recv.at[step, mask - 1],
                device_id=partner(stage, mask), device_id_type=MESH,
            )
            copy.start()
            out.append(copy)
        return out

    copies = []
    factors = []
    for m in range(2):
        factors.append(factor_last(m, f_copies[m]))
        term(m, (1 - core) * half, half)
        copies += [send(p, 0) for p in parts if reduce_parts[p][0] // rank == m]
    factor = jnp.concatenate(factors, axis=0)
    product = lax.dot_general(
        factor, jnp.concatenate([factor, factor], axis=0), NT,
        precision=lax.Precision.HIGHEST, preferred_element_type=F32,
    ) * 0.5
    lane = lax.broadcasted_iota(jnp.int32, (rank, LANES), 1)
    gram[0] = jnp.where(lane < rank, product[0:rank], product[rank : 2 * rank])
    g_copies = gram_send(0)
    for m in range(2):
        term(m, core * half, half)
    for step in range(nsteps):
        for p in parts:
            low, high, stages = reduce_parts[p]
            cuts, sizes, offsets = shape[p]
            size = sizes[step + 1]
            for copy in copies[p]:
                copy.wait()
            here = pl.ds(pl.multiple_of(starts[p][step + 1], LANES), size)
            members = 1 << len(stages[step])
            terms = [
                z_in[low:high, offsets[step] + i * size : offsets[step] + (i + 1) * size]
                for i in range(members - cuts[step])
            ]
            added = z[low:high, here] + terms[0] if cuts[step] else terms[0]
            for term_in in terms[1:]:
                added = added + term_in
            if step + 1 < nsteps:
                z[low:high, here] = added
                copies[p] = send(p, step + 1)
            else:
                total[low:high, here] = added
        for copy in g_copies:
            copy.wait()
        members = len(g_copies) + 1
        summed = gram_in[step, 0]
        for i in range(1, members):
            summed = summed + gram_in[step, i]
        gram[step + 1] = summed
        g_copies = gram_send(step + 1) if step + 1 < nsteps else []

    def back(p, step):
        low, high, stages = reduce_parts[p]
        cuts, sizes, _ = shape[p]
        if not cuts[step]:
            return []
        at = (pl.ds(low, high - low), pl.ds(pl.multiple_of(starts[p][step + 1], LANES), sizes[step + 1]))
        out = []
        for mask in masks(stages[step]):
            copy = pltpu.make_async_remote_copy(
                src_ref=total.at[at], dst_ref=total.at[at],
                send_sem=b_send.at[p, step, mask - 1], recv_sem=b_recv.at[p, step, mask - 1],
                device_id=partner(stages[step], mask), device_id_type=MESH,
            )
            copy.start()
            out.append(copy)
        return out

    def advance(step):
        for p in parts:
            for copy in copies[p]:
                copy.wait()
            copies[p] = back(p, step - 1) if step > 0 else []

    copies = [back(p, nsteps - 1) for p in parts]

    row = lax.broadcasted_iota(jnp.int32, (rank, LANES), 0)
    lane = lax.broadcasted_iota(jnp.int32, (rank, LANES), 1)
    first = lax.rem(lane, 2 * rank) < rank
    work = jnp.where(lane < 2 * rank, gram[nsteps], jnp.where(lax.rem(lane, rank) == row, 1.0, 0.0))
    for j in range(rank):
        if j == 12:
            advance(2)
        column = jnp.where(first, work[:, j : j + 1], work[:, rank + j : rank + j + 1])
        top = work[j : j + 1, :] / column[j : j + 1, :]
        work = jnp.where(row > j, work - column * top, work)
    pivots = [
        jnp.sum(jnp.where(lane == row + m * rank, work, 0.0), axis=1, keepdims=True) for m in range(2)
    ]
    scaled = work / jnp.sqrt(jnp.where(first, pivots[0], pivots[1]))
    inv = [scaled[:, (2 + m) * rank : (3 + m) * rank] for m in range(2)]
    for m in range(2):
        solved = lax.dot_general(
            inv[m], factor[m * rank : (m + 1) * rank, 0:rows], NN,
            precision=lax.Precision.HIGHEST, preferred_element_type=F32,
        )
        left_t[m * rank : (m + 1) * rank] = solved
        folded[m] = lax.dot_general(
            solved, inv[m], TN, precision=lax.Precision.HIGHEST, preferred_element_type=F32
        ) * (1.0 / replicas)

    advance(1)
    advance(0)
    own = pl.ds(pl.multiple_of(f * width, LANES), width)
    for m in range(2):
        at = slice(m * rank, (m + 1) * rank)
        own_basis[at] = dot32(inv[m], total[at, own], NN) * (1.0 / replicas)


def finish(merged, total, folded, left_in, basis_in, out, left_out, basis_out):
    rank = total.shape[0] // 2
    block = out.shape[2]
    here = pl.ds(pl.multiple_of(pl.program_id(0) * block, block), block)

    @pl.when(pl.program_id(0) == 0)
    def _():
        left_out[...] = left_in[...]
        basis_out[...] = basis_in[...]

    for m in range(2):
        approx = dot32(folded[m], total[m * rank : (m + 1) * rank, here], NN)
        out[m] = merged[m, :, here] - approx


def solution(mesh):
    n, replicas = mesh.shape["fsdp"], mesh.shape["replica"]
    nb, nr = log2(n), log2(replicas)

    def shards(grads, errors, basis):
        _, nmat, rows, cols = grads.shape
        width, _, rank = basis.shape
        grads, errors = grads[0], errors[0]
        basis_t = jnp.transpose(basis, (1, 2, 0)).reshape(nmat * rank, width)
        full = nmat * rank
        share = width // replicas >= LANES
        piece = width // replicas if share else width
        reduce_parts = plan(nb, nr, share)[0]
        nparts, steps = len(reduce_parts), 3
        most = max(1 << len(stage) for stage in reduce_parts[0][2])
        arrivals = max(offsets[-1] for _, _, offsets in layout(nb, nr, cols))
        vmem = pl.BlockSpec(memory_space=pltpu.VMEM)
        hbm = pl.BlockSpec(memory_space=pltpu.HBM)
        dma = pltpu.SemaphoreType.DMA
        merged, total, left_t, own_basis, folded = pl.pallas_call(
            functools.partial(exchange, n, replicas, share),
            out_shape=[
                pltpu.VMEM((nmat, rows, cols), F32),
                pltpu.VMEM((full, cols), F32),
                pltpu.VMEM((full, rows), F32),
                pltpu.VMEM((full, width), F32),
                pltpu.VMEM((nmat, rows, rank), F32),
            ],
            in_specs=[hbm, hbm, vmem],
            out_specs=[vmem] * 5,
            scratch_shapes=[
                pltpu.VMEM((2,) * (nb + nr * share) + (full, piece), F32),
                pltpu.VMEM((nmat, rows, cols), BF16),
                pltpu.VMEM((nmat, 2 * rows, cols), BF16),
                pltpu.VMEM((nmat, 2 * rank, 2 * rows), F32),
                pltpu.VMEM((nr + 1, nmat, rank, 2 * rows), F32),
                pltpu.VMEM((nr, nmat, rank, 2 * rows), F32),
                pltpu.VMEM((full, cols), F32),
                pltpu.VMEM((full, arrivals), F32),
                pltpu.VMEM((steps + 1, rank, LANES), F32),
                pltpu.VMEM((steps, most, rank, LANES), F32),
                dma((nmat, 2)),
                dma((2, 3, most)), dma((2, 3, most)),
                dma((nr, nmat)), dma((nr, nmat)),
                dma((nparts, steps, most)), dma((nparts, steps, most)),
                dma((steps, most)), dma((steps, most)),
                dma((nparts, steps, most)), dma((nparts, steps, most)),
            ],
            compiler_params=pltpu.CompilerParams(
                collective_id=0, has_side_effects=True, vmem_limit_bytes=56 * 1024 * 1024
            ),
        )(grads, errors, basis_t)

        block = 1024
        whole = lambda a: pl.BlockSpec(a.shape, lambda i: (0,) * a.ndim)
        new_errors, left_t, own_basis = pl.pallas_call(
            finish,
            grid=(cols // block,),
            out_shape=[
                jax.ShapeDtypeStruct((nmat, rows, cols), F32),
                jax.ShapeDtypeStruct(left_t.shape, F32),
                jax.ShapeDtypeStruct(own_basis.shape, F32),
            ],
            in_specs=[
                vmem,
                vmem,
                vmem,
                vmem,
                vmem,
            ],
            out_specs=[
                pl.BlockSpec((nmat, rows, block), lambda i: (0, 0, i)),
                whole(left_t),
                whole(own_basis),
            ],
            compiler_params=pltpu.CompilerParams(vmem_limit_bytes=24 * 1024 * 1024),
        )(merged, total, folded, left_t, own_basis)
        left = jnp.transpose(left_t.reshape(nmat, rank, rows), (0, 2, 1))
        new_basis = jnp.transpose(own_basis.reshape(nmat, rank, width), (2, 0, 1))
        return (new_errors[None], left, new_basis)

    in_specs = (
        P("replica", None, "fsdp", None),
        P("replica", None, "fsdp", None),
        P("fsdp", None, None),
    )
    out_specs = (P("replica", None, "fsdp", None), P(None, "fsdp", None), P("fsdp", None, None))
    return jax.shard_map(shards, mesh=mesh, in_specs=in_specs, out_specs=out_specs, check_vma=False)
```

```python
import functools

import jax
import jax.numpy as jnp
from jax import lax
from jax.experimental import pallas as pl
from jax.experimental.pallas import tpu as pltpu
from jax.sharding import PartitionSpec as P

MESH = pl.DeviceIdType.MESH
F32, BF16 = jnp.float32, jnp.bfloat16
TILE = 512
LANES = 128
NT = (((1,), (1,)), ((), ()))
NN = (((1,), (0,)), ((), ()))
TN = (((0,), (0,)), ((), ()))


def split(x):
    high = x.astype(BF16)
    return high, (x - high.astype(F32)).astype(BF16)


def dot32(a, b, dims):
    (ca,), (cb,) = dims[0]
    ah, al = split(a)
    bh, bl = split(b)
    left = jnp.concatenate([ah, ah, al], axis=ca)
    right = jnp.concatenate([bh, bl, bh], axis=cb)
    return lax.dot_general(left, right, dims, preferred_element_type=F32)


def log2(n):
    return n.bit_length() - 1


def plan(nb, nr, share):
    core, near = [("fsdp", 0)], [("fsdp", 1)]
    far = [("fsdp", b) for b in range(2, nb)]
    across = [("replica", b) for b in range(nr)]
    plane_first = [core, near + across, far]
    far_first = [core, far, near + across]
    reduce_parts = [
        (0, 16, plane_first), (16, 32, plane_first), (32, 40, plane_first),
        (40, 48, far_first), (48, 64, far_first),
    ]
    plane = near + across if share else near
    gather_parts = [(0, 40, [far, plane, core]), (40, 64, [plane, far, core])]
    return reduce_parts, gather_parts


def layout(nb, nr, cols):
    out = []
    for _, _, stages in plan(nb, nr, False)[0]:
        cuts, sizes, offsets = [], [cols], [0]
        for stage in stages:
            members = 1 << len(stage)
            cuts.append(sizes[-1] // members >= LANES)
            sizes.append(sizes[-1] // members if cuts[-1] else sizes[-1])
            offsets.append(offsets[-1] + (members - cuts[-1]) * sizes[-1])
        out.append((cuts, sizes, offsets))
    return out


def exchange(
    n, replicas, share, grads, errors, basis, merged, total, left_t, own_basis, folded,
    held, g_buf, mhl, acc, ft, ft_in, z, z_in, gram, gram_in,
    load_sem, a_send, a_recv, f_send, f_recv, s_send, s_recv, m_send, m_recv, b_send, b_recv,
):
    nb, nr = log2(n), log2(replicas)
    reduce_parts, gather_parts = plan(nb, nr, share)
    rank = basis.shape[0] // 2
    width = basis.shape[1]
    rows = grads.shape[1]
    cols = grads.shape[2]
    y, f = lax.axis_index("replica"), lax.axis_index("fsdp")

    def bit_of(link):
        return lax.rem(lax.div(f if link[0] == "fsdp" else y, 1 << link[1]), 2)

    def index_of(stage, mask=0):
        total_index = 0
        for i, link in enumerate(stage):
            own = bit_of(link)
            total_index = total_index + (1 - own if mask >> i & 1 else own) * (1 << i)
        return total_index

    def partner(stage, mask):
        there = {"replica": y, "fsdp": f}
        for i, link in enumerate(stage):
            if mask >> i & 1:
                there[link[0]] = there[link[0]] + (1 - 2 * bit_of(link)) * (1 << link[1])
        return (there["replica"], there["fsdp"])

    def masks(stage):
        return range(1, 1 << len(stage))

    loads = [
        [
            pltpu.make_async_copy(grads.at[m], g_buf.at[m], load_sem.at[m, 0]),
            pltpu.make_async_copy(errors.at[m], merged.at[m], load_sem.at[m, 1]),
        ]
        for m in range(2)
    ]
    for load in loads[0] + loads[1]:
        load.start()

    barrier = pltpu.get_barrier_semaphore()
    peers = [(stage, mask) for stage in reduce_parts[0][2] for mask in masks(stage)]
    for stage, mask in peers:
        pl.semaphore_signal(barrier, inc=1, device_id=partner(stage, mask), device_id_type=MESH)
    held_links = [("fsdp", b) for b in range(nb - 1, -1, -1)]
    if share:
        held_links += [("replica", b) for b in range(nr - 1, -1, -1)]
    piece = held.shape[-1]
    mine = tuple(bit_of(link) for link in held_links)
    first_column = sum(bit_of(link) * (1 << link[1]) for link in held_links if link[0] == "replica") * piece
    if share:
        held[mine] = basis[:, pl.ds(pl.multiple_of(first_column, LANES), piece)]
    else:
        held[mine] = basis[...]
    pl.semaphore_wait(barrier, len(peers))

    def gather_copy(part, step, at, mask, slot):
        low, high, stages = gather_parts[part]
        ref = held.at[at + (pl.ds(low, high - low), slice(None))]
        copy = pltpu.make_async_remote_copy(
            src_ref=ref, dst_ref=ref,
            send_sem=a_send.at[part, step, slot], recv_sem=a_recv.at[part, step, slot],
            device_id=partner(stages[step], mask), device_id_type=MESH,
        )
        copy.start()
        return copy

    def gather(part, step):
        stages = gather_parts[part][2]
        done = [link for stage in stages[:step] for link in stage]
        at = tuple(slice(None) if link in done else bit_of(link) for link in held_links)
        return [gather_copy(part, step, at, mask, mask - 1) for mask in masks(stages[step])]

    def pass_on(part, mask):
        first_stage, second_stage, _ = gather_parts[part][2]
        at = []
        for link in held_links:
            own = bit_of(link)
            if link in first_stage:
                own = slice(None)
            elif link in second_stage and mask >> second_stage.index(link) & 1:
                own = 1 - own
            at.append(own)
        return gather_copy(part, 2, tuple(at), 1, mask)

    def factor_tiles(m, free, begin):
        end = 1 << len(free)
        group = 8 if begin % 8 == 0 and end % 8 == 0 else 4

        @pl.loop(begin // group, end // group)
        def _(outer):
            summed = 0.0
            for inner in range(group):
                j = outer * group + inner
                bits = []
                for link in held_links:
                    own = bit_of(link)
                    if link in free:
                        flip = lax.rem(lax.div(j, 1 << free.index(link)), 2)
                        own = own + flip * (1 - 2 * own)
                    bits.append(own)
                start = 0
                for link, value in zip(held_links, bits):
                    start = start + value * ((1 << link[1]) * (width if link[0] == "fsdp" else piece))
                here = pl.ds(pl.multiple_of(start, LANES), piece)
                high, low = split(held[tuple(bits) + (pl.ds(m * rank, rank), slice(None))])
                summed = summed + lax.dot_general(
                    jnp.concatenate([high, low], axis=0), mhl[m, :, here], NT, preferred_element_type=F32
                )
            acc[m] += summed

    copies = [gather(part, 0) for part in range(2)]
    acc[...] = jnp.zeros_like(acc)

    def convert(m):
        for load in loads[m]:
            load.wait()

        @pl.loop(0, cols // (2 * TILE))
        def _(t):
            here = pl.ds(pl.multiple_of(t * 2 * TILE, 2 * TILE), 2 * TILE)
            both = g_buf[m, :, here].astype(F32) + merged[m, :, here]
            merged[m, :, here] = both
            high, low = split(both)
            mhl[m, 0:rows, here] = high
            mhl[m, rows : 2 * rows, here] = low

    one, two, three = gather_parts[0][2]

    passed = [[], []]

    def arrive(part, step):
        if step == 0:
            for copy in copies[part]:
                copy.wait()
            copies[part] = gather(part, 1)
            passed[part].append(pass_on(part, 0))
        elif step == 1:
            for mask, copy in enumerate(copies[part], 1):
                copy.wait_recv()
                passed[part].append(pass_on(part, mask))
            for copy in copies[part]:
                copy.wait_send()
        else:
            for copy in passed[part]:
                copy.wait()

    def factor_send(m, b):
        copy = pltpu.make_async_remote_copy(
            src_ref=ft.at[b, m], dst_ref=ft_in.at[b, m],
            send_sem=f_send.at[b, m], recv_sem=f_recv.at[b, m],
            device_id=partner([("replica", b)], 1), device_id_type=MESH,
        )
        copy.start()
        return copy

    def factor_first(m):
        factor_tiles(m, one + two + three, 1 << len(one + two))
        whole = acc[m, 0:rank] + acc[m, rank : 2 * rank]
        single = whole[:, 0:rows] + whole[:, rows : 2 * rows]
        ft[0, m] = jnp.concatenate([single, single], axis=1)
        return factor_send(m, 0)

    def factor_last(m, copy):
        for b in range(nr):
            copy.wait()
            ft[b + 1, m] = ft[b, m] + ft_in[b, m]
            if b + 1 < nr:
                copy = factor_send(m, b + 1)
        return ft[nr, m] * (1.0 / replicas)

    convert(0)
    for part in range(2):
        arrive(part, 0)
    convert(1)
    factor_tiles(0, one, 0)
    for part in range(2):
        arrive(part, 1)
    factor_tiles(0, one + two, 1 << len(one))
    factor_tiles(1, one + two, 0)
    arrive(0, 2)
    f_copies = [factor_first(0)]
    arrive(1, 2)
    f_copies.append(factor_first(1))

    def term(m, start, count):
        high, low = split(factors[m])
        weights = jnp.concatenate([high, low], axis=0)

        @pl.loop(0, count // (4 * TILE))
        def _(t):
            here = pl.ds(pl.multiple_of(start + t * 4 * TILE, 4 * TILE), 4 * TILE)
            out = lax.dot_general(weights, mhl[m, :, here], NN, preferred_element_type=F32)
            z[m * rank : (m + 1) * rank, here] = out[0:rank] + out[rank : 2 * rank]

    half = cols // 2
    core = bit_of(("fsdp", 0))
    parts = range(len(reduce_parts))
    nsteps = 3
    shape = layout(nb, nr, cols)
    starts = [[0] for _ in parts]

    def send(p, step):
        low, high, stages = reduce_parts[p]
        cuts, sizes, offsets = shape[p]
        stage, size, start = stages[step], sizes[step + 1], starts[p][step]
        place = index_of(stage)
        starts[p].append(start + place * size if cuts[step] else start)
        if not cuts[step]:
            own_at = pl.multiple_of(offsets[step] + place * size, LANES)
            z_in[low:high, pl.ds(own_at, size)] = z[low:high, pl.ds(pl.multiple_of(start, LANES), size)]
        out = []
        for mask in masks(stage):
            if cuts[step]:
                away, land = start + index_of(stage, mask) * size, offsets[step] + (mask - 1) * size
            else:
                away, land = start, offsets[step] + place * size
            copy = pltpu.make_async_remote_copy(
                src_ref=z.at[pl.ds(low, high - low), pl.ds(pl.multiple_of(away, LANES), size)],
                dst_ref=z_in.at[pl.ds(low, high - low), pl.ds(pl.multiple_of(land, LANES), size)],
                send_sem=s_send.at[p, step, mask - 1], recv_sem=s_recv.at[p, step, mask - 1],
                device_id=partner(stage, mask), device_id_type=MESH,
            )
            copy.start()
            out.append(copy)
        return out

    def gram_send(step):
        stage = [link for link in reduce_parts[0][2][step] if link[0] == "fsdp"]
        place = index_of(stage)
        gram_in[step, place] = gram[step]
        out = []
        for mask in masks(stage):
            copy = pltpu.make_async_remote_copy(
                src_ref=gram.at[step], dst_ref=gram_in.at[step, place],
                send_sem=m_send.at[step, mask - 1], recv_sem=m_recv.at[step, mask - 1],
                device_id=partner(stage, mask), device_id_type=MESH,
            )
            copy.start()
            out.append(copy)
        return out

    copies = []
    factors = []
    for m in range(2):
        factors.append(factor_last(m, f_copies[m]))
        term(m, (1 - core) * half, half)
        copies += [send(p, 0) for p in parts if reduce_parts[p][0] // rank == m]
    factor = jnp.concatenate(factors, axis=0)
    product = lax.dot_general(
        factor, jnp.concatenate([factor, factor], axis=0), NT,
        precision=lax.Precision.HIGHEST, preferred_element_type=F32,
    ) * 0.5
    lane = lax.broadcasted_iota(jnp.int32, (rank, LANES), 1)
    gram[0] = jnp.where(lane < rank, product[0:rank], product[rank : 2 * rank])
    g_copies = gram_send(0)
    for m in range(2):
        term(m, core * half, half)
    for step in range(nsteps):
        for p in parts:
            low, high, stages = reduce_parts[p]
            cuts, sizes, offsets = shape[p]
            size = sizes[step + 1]
            for copy in copies[p]:
                copy.wait()
            here = pl.ds(pl.multiple_of(starts[p][step + 1], LANES), size)
            members = 1 << len(stages[step])
            terms = [
                z_in[low:high, offsets[step] + i * size : offsets[step] + (i + 1) * size]
                for i in range(members - cuts[step])
            ]
            added = z[low:high, here] + terms[0] if cuts[step] else terms[0]
            for term_in in terms[1:]:
                added = added + term_in
            if step + 1 < nsteps:
                z[low:high, here] = added
                copies[p] = send(p, step + 1)
            else:
                total[low:high, here] = added
        for copy in g_copies:
            copy.wait()
        members = len(g_copies) + 1
        summed = gram_in[step, 0]
        for i in range(1, members):
            summed = summed + gram_in[step, i]
        gram[step + 1] = summed
        g_copies = gram_send(step + 1) if step + 1 < nsteps else []

    def back_copy(p, step, start, size, mask, slot):
        low, high, stages = reduce_parts[p]
        ref = total.at[pl.ds(low, high - low), pl.ds(pl.multiple_of(start, LANES), size)]
        copy = pltpu.make_async_remote_copy(
            src_ref=ref, dst_ref=ref,
            send_sem=b_send.at[p, step, slot], recv_sem=b_recv.at[p, step, slot],
            device_id=partner(stages[step], mask), device_id_type=MESH,
        )
        copy.start()
        return copy

    def back(p, step):
        cuts, sizes, _ = shape[p]
        if not cuts[step]:
            return []
        return [
            back_copy(p, step, starts[p][step + 1], sizes[step + 1], mask, mask - 1)
            for mask in masks(reduce_parts[p][2][step])
        ]

    handed = [[] for _ in parts]

    def advance(step):
        for p in parts:
            sizes, stages = shape[p][1], reduce_parts[p][2]
            if step == 2:
                for copy in copies[p]:
                    copy.wait()
                copies[p] = back(p, 1)
                handed[p].append(back_copy(p, 0, starts[p][2], sizes[2], 1, 0))
            elif step == 1:
                for mask, copy in enumerate(copies[p], 1):
                    copy.wait_recv()
                    start = starts[p][1] + index_of(stages[1], mask) * sizes[2]
                    handed[p].append(back_copy(p, 0, start, sizes[2], 1, mask))
                for copy in copies[p]:
                    copy.wait_send()
            else:
                for copy in handed[p]:
                    copy.wait()

    copies = [back(p, nsteps - 1) for p in parts]

    row = lax.broadcasted_iota(jnp.int32, (rank, LANES), 0)
    lane = lax.broadcasted_iota(jnp.int32, (rank, LANES), 1)
    first = lax.rem(lane, 2 * rank) < rank
    work = jnp.where(lane < 2 * rank, gram[nsteps], jnp.where(lax.rem(lane, rank) == row, 1.0, 0.0))
    for j in range(rank):
        if j == 12:
            advance(2)
        column = jnp.where(first, work[:, j : j + 1], work[:, rank + j : rank + j + 1])
        top = work[j : j + 1, :] / column[j : j + 1, :]
        work = jnp.where(row > j, work - column * top, work)
    pivots = [
        jnp.sum(jnp.where(lane == row + m * rank, work, 0.0), axis=1, keepdims=True) for m in range(2)
    ]
    scaled = work / jnp.sqrt(jnp.where(first, pivots[0], pivots[1]))
    inv = [scaled[:, (2 + m) * rank : (3 + m) * rank] for m in range(2)]
    for m in range(2):
        solved = lax.dot_general(
            inv[m], factor[m * rank : (m + 1) * rank, 0:rows], NN,
            precision=lax.Precision.HIGHEST, preferred_element_type=F32,
        )
        left_t[m * rank : (m + 1) * rank] = solved
        folded[m] = lax.dot_general(
            solved, inv[m], TN, precision=lax.Precision.HIGHEST, preferred_element_type=F32
        ) * (1.0 / replicas)

    advance(1)
    advance(0)
    own = pl.ds(pl.multiple_of(f * width, LANES), width)
    for m in range(2):
        at = slice(m * rank, (m + 1) * rank)
        own_basis[at] = dot32(inv[m], total[at, own], NN) * (1.0 / replicas)


def finish(merged, total, folded, left_in, basis_in, out, left_out, basis_out):
    rank = total.shape[0] // 2
    block = out.shape[2]
    here = pl.ds(pl.multiple_of(pl.program_id(0) * block, block), block)

    @pl.when(pl.program_id(0) == 0)
    def _():
        left_out[...] = left_in[...]
        basis_out[...] = basis_in[...]

    for m in range(2):
        approx = dot32(folded[m], total[m * rank : (m + 1) * rank, here], NN)
        out[m] = merged[m, :, here] - approx


def solution(mesh):
    n, replicas = mesh.shape["fsdp"], mesh.shape["replica"]
    nb, nr = log2(n), log2(replicas)

    def shards(grads, errors, basis):
        _, nmat, rows, cols = grads.shape
        width, _, rank = basis.shape
        grads, errors = grads[0], errors[0]
        basis_t = jnp.transpose(basis, (1, 2, 0)).reshape(nmat * rank, width)
        full = nmat * rank
        share = width // replicas >= LANES
        piece = width // replicas if share else width
        reduce_parts = plan(nb, nr, share)[0]
        nparts, steps = len(reduce_parts), 3
        most = max(1 << len(stage) for stage in reduce_parts[0][2])
        arrivals = max(offsets[-1] for _, _, offsets in layout(nb, nr, cols))
        vmem = pl.BlockSpec(memory_space=pltpu.VMEM)
        hbm = pl.BlockSpec(memory_space=pltpu.HBM)
        dma = pltpu.SemaphoreType.DMA
        merged, total, left_t, own_basis, folded = pl.pallas_call(
            functools.partial(exchange, n, replicas, share),
            out_shape=[
                pltpu.VMEM((nmat, rows, cols), F32),
                pltpu.VMEM((full, cols), F32),
                pltpu.VMEM((full, rows), F32),
                pltpu.VMEM((full, width), F32),
                pltpu.VMEM((nmat, rows, rank), F32),
            ],
            in_specs=[hbm, hbm, vmem],
            out_specs=[vmem] * 5,
            scratch_shapes=[
                pltpu.VMEM((2,) * (nb + nr * share) + (full, piece), F32),
                pltpu.VMEM((nmat, rows, cols), BF16),
                pltpu.VMEM((nmat, 2 * rows, cols), BF16),
                pltpu.VMEM((nmat, 2 * rank, 2 * rows), F32),
                pltpu.VMEM((nr + 1, nmat, rank, 2 * rows), F32),
                pltpu.VMEM((nr, nmat, rank, 2 * rows), F32),
                pltpu.VMEM((full, cols), F32),
                pltpu.VMEM((full, arrivals), F32),
                pltpu.VMEM((steps + 1, rank, LANES), F32),
                pltpu.VMEM((steps, most, rank, LANES), F32),
                dma((nmat, 2)),
                dma((2, 3, most)), dma((2, 3, most)),
                dma((nr, nmat)), dma((nr, nmat)),
                dma((nparts, steps, most)), dma((nparts, steps, most)),
                dma((steps, most)), dma((steps, most)),
                dma((nparts, steps, most)), dma((nparts, steps, most)),
            ],
            compiler_params=pltpu.CompilerParams(
                collective_id=0, has_side_effects=True, vmem_limit_bytes=56 * 1024 * 1024
            ),
        )(grads, errors, basis_t)

        block = 1024
        whole = lambda a: pl.BlockSpec(a.shape, lambda i: (0,) * a.ndim)
        new_errors, left_t, own_basis = pl.pallas_call(
            finish,
            grid=(cols // block,),
            out_shape=[
                jax.ShapeDtypeStruct((nmat, rows, cols), F32),
                jax.ShapeDtypeStruct(left_t.shape, F32),
                jax.ShapeDtypeStruct(own_basis.shape, F32),
            ],
            in_specs=[
                vmem,
                vmem,
                vmem,
                vmem,
                vmem,
            ],
            out_specs=[
                pl.BlockSpec((nmat, rows, block), lambda i: (0, 0, i)),
                whole(left_t),
                whole(own_basis),
            ],
            compiler_params=pltpu.CompilerParams(vmem_limit_bytes=24 * 1024 * 1024),
        )(merged, total, folded, left_t, own_basis)
        left = jnp.transpose(left_t.reshape(nmat, rank, rows), (0, 2, 1))
        new_basis = jnp.transpose(own_basis.reshape(nmat, rank, width), (2, 0, 1))
        return (new_errors[None], left, new_basis)

    in_specs = (
        P("replica", None, "fsdp", None),
        P("replica", None, "fsdp", None),
        P("fsdp", None, None),
    )
    out_specs = (P("replica", None, "fsdp", None), P(None, "fsdp", None), P("fsdp", None, None))
    return jax.shard_map(shards, mesh=mesh, in_specs=in_specs, out_specs=out_specs, check_vma=False)
```

```python
import functools

import jax
import jax.numpy as jnp
from jax import lax
from jax.experimental import pallas as pl
from jax.experimental.pallas import tpu as pltpu
from jax.sharding import PartitionSpec as P

MESH = pl.DeviceIdType.MESH
F32, BF16 = jnp.float32, jnp.bfloat16
TILE = 512
LANES = 128
NT = (((1,), (1,)), ((), ()))
NN = (((1,), (0,)), ((), ()))
TN = (((0,), (0,)), ((), ()))


def split(x):
    high = x.astype(BF16)
    return high, (x - high.astype(F32)).astype(BF16)


def dot32(a, b, dims):
    (ca,), (cb,) = dims[0]
    ah, al = split(a)
    bh, bl = split(b)
    left = jnp.concatenate([ah, ah, al], axis=ca)
    right = jnp.concatenate([bh, bl, bh], axis=cb)
    return lax.dot_general(left, right, dims, preferred_element_type=F32)


def log2(n):
    return n.bit_length() - 1


def plan(nb, nr, share):
    core, near = [("fsdp", 0)], [("fsdp", 1)]
    far = [("fsdp", b) for b in range(2, nb)]
    across = [("replica", b) for b in range(nr)]
    x_first = [core, near, across, far]
    y_first = [core, across, near, far]
    z_first = [core, far[:1], far[1:], near + across]
    reduce_parts = [
        (0, 8, x_first), (8, 24, x_first), (24, 32, z_first),
        (32, 40, z_first), (40, 48, y_first), (48, 64, y_first),
    ]
    plane = near + across if share else near
    gather_parts = [(0, 40, [far, plane, core]), (40, 64, [plane, far, core])]
    return reduce_parts, gather_parts


def layout(nb, nr, cols):
    out = []
    for _, _, stages in plan(nb, nr, False)[0]:
        cuts, sizes, offsets = [], [cols], [0]
        for stage in stages:
            members = 1 << len(stage)
            cuts.append(sizes[-1] // members >= LANES)
            sizes.append(sizes[-1] // members if cuts[-1] else sizes[-1])
            offsets.append(offsets[-1] + (members - cuts[-1]) * sizes[-1])
        out.append((cuts, sizes, offsets))
    return out


def exchange(
    n, replicas, share, grads, errors, basis, merged, total, left_t, own_basis, folded,
    held, g_buf, mhl, acc, ft, ft_in, z, z_in, gram, gram_in,
    load_sem, a_send, a_recv, f_send, f_recv, s_send, s_recv, m_send, m_recv, b_send, b_recv,
):
    nb, nr = log2(n), log2(replicas)
    reduce_parts, gather_parts = plan(nb, nr, share)
    rank = basis.shape[0] // 2
    width = basis.shape[1]
    rows = grads.shape[1]
    cols = grads.shape[2]
    y, f = lax.axis_index("replica"), lax.axis_index("fsdp")

    def bit_of(link):
        return lax.rem(lax.div(f if link[0] == "fsdp" else y, 1 << link[1]), 2)

    def index_of(stage, mask=0):
        total_index = 0
        for i, link in enumerate(stage):
            own = bit_of(link)
            total_index = total_index + (1 - own if mask >> i & 1 else own) * (1 << i)
        return total_index

    def partner(stage, mask):
        there = {"replica": y, "fsdp": f}
        for i, link in enumerate(stage):
            if mask >> i & 1:
                there[link[0]] = there[link[0]] + (1 - 2 * bit_of(link)) * (1 << link[1])
        return (there["replica"], there["fsdp"])

    def masks(stage):
        return range(1, 1 << len(stage))

    loads = [
        [
            pltpu.make_async_copy(grads.at[m], g_buf.at[m], load_sem.at[m, 0]),
            pltpu.make_async_copy(errors.at[m], merged.at[m], load_sem.at[m, 1]),
        ]
        for m in range(2)
    ]
    for load in loads[0] + loads[1]:
        load.start()

    barrier = pltpu.get_barrier_semaphore()
    groups = [[("fsdp", 0)], [("fsdp", 1)] + [("replica", b) for b in range(nr)], [("fsdp", b) for b in range(2, nb)]]
    peers = [(group, mask) for group in groups for mask in masks(group)]
    for stage, mask in peers:
        pl.semaphore_signal(barrier, inc=1, device_id=partner(stage, mask), device_id_type=MESH)
    held_links = [("fsdp", b) for b in range(nb - 1, -1, -1)]
    if share:
        held_links += [("replica", b) for b in range(nr - 1, -1, -1)]
    piece = held.shape[-1]
    mine = tuple(bit_of(link) for link in held_links)
    first_column = sum(bit_of(link) * (1 << link[1]) for link in held_links if link[0] == "replica") * piece
    if share:
        held[mine] = basis[:, pl.ds(pl.multiple_of(first_column, LANES), piece)]
    else:
        held[mine] = basis[...]
    pl.semaphore_wait(barrier, len(peers))

    def gather_copy(part, step, at, mask, slot):
        low, high, stages = gather_parts[part]
        ref = held.at[at + (pl.ds(low, high - low), slice(None))]
        copy = pltpu.make_async_remote_copy(
            src_ref=ref, dst_ref=ref,
            send_sem=a_send.at[part, step, slot], recv_sem=a_recv.at[part, step, slot],
            device_id=partner(stages[step], mask), device_id_type=MESH,
        )
        copy.start()
        return copy

    def gather(part, step):
        stages = gather_parts[part][2]
        done = [link for stage in stages[:step] for link in stage]
        at = tuple(slice(None) if link in done else bit_of(link) for link in held_links)
        return [gather_copy(part, step, at, mask, mask - 1) for mask in masks(stages[step])]

    def pass_on(part, mask):
        first_stage, second_stage, _ = gather_parts[part][2]
        at = []
        for link in held_links:
            own = bit_of(link)
            if link in first_stage:
                own = slice(None)
            elif link in second_stage and mask >> second_stage.index(link) & 1:
                own = 1 - own
            at.append(own)
        return gather_copy(part, 2, tuple(at), 1, mask)

    def factor_tiles(m, free, begin):
        end = 1 << len(free)
        group = 8 if begin % 8 == 0 and end % 8 == 0 else 4

        @pl.loop(begin // group, end // group)
        def _(outer):
            summed = 0.0
            for inner in range(group):
                j = outer * group + inner
                bits = []
                for link in held_links:
                    own = bit_of(link)
                    if link in free:
                        flip = lax.rem(lax.div(j, 1 << free.index(link)), 2)
                        own = own + flip * (1 - 2 * own)
                    bits.append(own)
                start = 0
                for link, value in zip(held_links, bits):
                    start = start + value * ((1 << link[1]) * (width if link[0] == "fsdp" else piece))
                here = pl.ds(pl.multiple_of(start, LANES), piece)
                high, low = split(held[tuple(bits) + (pl.ds(m * rank, rank), slice(None))])
                summed = summed + lax.dot_general(
                    jnp.concatenate([high, low], axis=0), mhl[m, :, here], NT, preferred_element_type=F32
                )
            acc[m] += summed

    copies = [gather(part, 0) for part in range(2)]
    acc[...] = jnp.zeros_like(acc)

    def convert(m):
        for load in loads[m]:
            load.wait()

        @pl.loop(0, cols // (2 * TILE))
        def _(t):
            here = pl.ds(pl.multiple_of(t * 2 * TILE, 2 * TILE), 2 * TILE)
            both = g_buf[m, :, here].astype(F32) + merged[m, :, here]
            merged[m, :, here] = both
            high, low = split(both)
            mhl[m, 0:rows, here] = high
            mhl[m, rows : 2 * rows, here] = low

    one, two, three = gather_parts[0][2]

    passed = [[], []]

    def arrive(part, step):
        if step == 0:
            for copy in copies[part]:
                copy.wait()
            copies[part] = gather(part, 1)
            passed[part].append(pass_on(part, 0))
        elif step == 1:
            for mask, copy in enumerate(copies[part], 1):
                copy.wait_recv()
                passed[part].append(pass_on(part, mask))
            for copy in copies[part]:
                copy.wait_send()
        else:
            for copy in passed[part]:
                copy.wait()

    def factor_send(m, b):
        copy = pltpu.make_async_remote_copy(
            src_ref=ft.at[b, m], dst_ref=ft_in.at[b, m],
            send_sem=f_send.at[b, m], recv_sem=f_recv.at[b, m],
            device_id=partner([("replica", b)], 1), device_id_type=MESH,
        )
        copy.start()
        return copy

    def factor_first(m):
        factor_tiles(m, one + two + three, 1 << len(one + two))
        whole = acc[m, 0:rank] + acc[m, rank : 2 * rank]
        single = whole[:, 0:rows] + whole[:, rows : 2 * rows]
        ft[0, m] = jnp.concatenate([single, single], axis=1)
        return factor_send(m, 0)

    def factor_last(m, copy):
        for b in range(nr):
            copy.wait()
            ft[b + 1, m] = ft[b, m] + ft_in[b, m]
            if b + 1 < nr:
                copy = factor_send(m, b + 1)
        return ft[nr, m] * (1.0 / replicas)

    convert(0)
    for part in range(2):
        arrive(part, 0)
    convert(1)
    factor_tiles(0, one, 0)
    for part in range(2):
        arrive(part, 1)
    factor_tiles(0, one + two, 1 << len(one))
    factor_tiles(1, one + two, 0)
    arrive(0, 2)
    f_copies = [factor_first(0)]
    arrive(1, 2)
    f_copies.append(factor_first(1))

    def term(m, start, count):
        high, low = split(factors[m])
        weights = jnp.concatenate([high, low], axis=0)

        @pl.loop(0, count // (4 * TILE))
        def _(t):
            here = pl.ds(pl.multiple_of(start + t * 4 * TILE, 4 * TILE), 4 * TILE)
            out = lax.dot_general(weights, mhl[m, :, here], NN, preferred_element_type=F32)
            z[m * rank : (m + 1) * rank, here] = out[0:rank] + out[rank : 2 * rank]

    half = cols // 2
    core = bit_of(("fsdp", 0))
    parts = range(len(reduce_parts))
    nsteps = len(reduce_parts[0][2])
    shape = layout(nb, nr, cols)
    starts = [[0] for _ in parts]

    def send(p, step):
        low, high, stages = reduce_parts[p]
        cuts, sizes, offsets = shape[p]
        stage, size, start = stages[step], sizes[step + 1], starts[p][step]
        place = index_of(stage)
        starts[p].append(start + place * size if cuts[step] else start)
        if not cuts[step]:
            own_at = pl.multiple_of(offsets[step] + place * size, LANES)
            z_in[low:high, pl.ds(own_at, size)] = z[low:high, pl.ds(pl.multiple_of(start, LANES), size)]
        out = []
        for mask in masks(stage):
            if cuts[step]:
                away, land = start + index_of(stage, mask) * size, offsets[step] + (mask - 1) * size
            else:
                away, land = start, offsets[step] + place * size
            copy = pltpu.make_async_remote_copy(
                src_ref=z.at[pl.ds(low, high - low), pl.ds(pl.multiple_of(away, LANES), size)],
                dst_ref=z_in.at[pl.ds(low, high - low), pl.ds(pl.multiple_of(land, LANES), size)],
                send_sem=s_send.at[p, step, mask - 1], recv_sem=s_recv.at[p, step, mask - 1],
                device_id=partner(stage, mask), device_id_type=MESH,
            )
            copy.start()
            out.append(copy)
        return out

    def gram_send(step):
        stage = [link for link in reduce_parts[0][2][step] if link[0] == "fsdp"]
        place = index_of(stage)
        gram_in[step, place] = gram[step]
        out = []
        for mask in masks(stage):
            copy = pltpu.make_async_remote_copy(
                src_ref=gram.at[step], dst_ref=gram_in.at[step, place],
                send_sem=m_send.at[step, mask - 1], recv_sem=m_recv.at[step, mask - 1],
                device_id=partner(stage, mask), device_id_type=MESH,
            )
            copy.start()
            out.append(copy)
        return out

    copies = []
    factors = []
    for m in range(2):
        factors.append(factor_last(m, f_copies[m]))
        term(m, (1 - core) * half, half)
        copies += [send(p, 0) for p in parts if reduce_parts[p][0] // rank == m]
    factor = jnp.concatenate(factors, axis=0)
    product = lax.dot_general(
        factor, jnp.concatenate([factor, factor], axis=0), NT,
        precision=lax.Precision.HIGHEST, preferred_element_type=F32,
    ) * 0.5
    lane = lax.broadcasted_iota(jnp.int32, (rank, LANES), 1)
    gram[0] = jnp.where(lane < rank, product[0:rank], product[rank : 2 * rank])
    g_copies = gram_send(0)
    for m in range(2):
        term(m, core * half, half)
    for step in range(nsteps):
        for p in parts:
            low, high, stages = reduce_parts[p]
            cuts, sizes, offsets = shape[p]
            size = sizes[step + 1]
            for copy in copies[p]:
                copy.wait()
            here = pl.ds(pl.multiple_of(starts[p][step + 1], LANES), size)
            members = 1 << len(stages[step])
            terms = [
                z_in[low:high, offsets[step] + i * size : offsets[step] + (i + 1) * size]
                for i in range(members - cuts[step])
            ]
            added = z[low:high, here] + terms[0] if cuts[step] else terms[0]
            for term_in in terms[1:]:
                added = added + term_in
            if step + 1 < nsteps:
                z[low:high, here] = added
                copies[p] = send(p, step + 1)
            else:
                total[low:high, here] = added
        for copy in g_copies:
            copy.wait()
        members = len(g_copies) + 1
        summed = gram_in[step, 0]
        for i in range(1, members):
            summed = summed + gram_in[step, i]
        gram[step + 1] = summed
        g_copies = gram_send(step + 1) if step + 1 < nsteps else []

    def back_copy(p, step, start, size, mask, slot):
        low, high, stages = reduce_parts[p]
        ref = total.at[pl.ds(low, high - low), pl.ds(pl.multiple_of(start, LANES), size)]
        copy = pltpu.make_async_remote_copy(
            src_ref=ref, dst_ref=ref,
            send_sem=b_send.at[p, step, slot], recv_sem=b_recv.at[p, step, slot],
            device_id=partner(stages[step], mask), device_id_type=MESH,
        )
        copy.start()
        return copy

    def back(p, step):
        cuts, sizes, _ = shape[p]
        if not cuts[step]:
            return []
        return [
            back_copy(p, step, starts[p][step + 1], sizes[step + 1], mask, mask - 1)
            for mask in masks(reduce_parts[p][2][step])
        ]

    handed = [[] for _ in parts]

    def hand(p, start, size):
        handed[p].append(back_copy(p, 0, start, size, 1, len(handed[p])))

    def advance(step):
        for p in parts:
            sizes, stages = shape[p][1], reduce_parts[p][2]
            if step == 0:
                for copy in handed[p]:
                    copy.wait()
                continue
            for mask, copy in enumerate(copies[p], 1):
                copy.wait_recv()
                hand(p, starts[p][step] + index_of(stages[step], mask) * sizes[step + 1], sizes[step + 1])
            for copy in copies[p]:
                copy.wait_send()
            copies[p] = back(p, step - 1) if step > 1 else []

    copies = [back(p, nsteps - 1) for p in parts]
    for p in parts:
        hand(p, starts[p][nsteps], shape[p][1][nsteps])

    row = lax.broadcasted_iota(jnp.int32, (rank, LANES), 0)
    lane = lax.broadcasted_iota(jnp.int32, (rank, LANES), 1)
    first = lax.rem(lane, 2 * rank) < rank
    work = jnp.where(lane < 2 * rank, gram[nsteps], jnp.where(lax.rem(lane, rank) == row, 1.0, 0.0))
    for j in range(rank):
        if j == 10:
            advance(3)
        if j == 22:
            advance(2)
        column = jnp.where(first, work[:, j : j + 1], work[:, rank + j : rank + j + 1])
        top = work[j : j + 1, :] / column[j : j + 1, :]
        work = jnp.where(row > j, work - column * top, work)
    pivots = [
        jnp.sum(jnp.where(lane == row + m * rank, work, 0.0), axis=1, keepdims=True) for m in range(2)
    ]
    scaled = work / jnp.sqrt(jnp.where(first, pivots[0], pivots[1]))
    inv = [scaled[:, (2 + m) * rank : (3 + m) * rank] for m in range(2)]
    for m in range(2):
        solved = lax.dot_general(
            inv[m], factor[m * rank : (m + 1) * rank, 0:rows], NN,
            precision=lax.Precision.HIGHEST, preferred_element_type=F32,
        )
        left_t[m * rank : (m + 1) * rank] = solved
        folded[m] = lax.dot_general(
            solved, inv[m], TN, precision=lax.Precision.HIGHEST, preferred_element_type=F32
        ) * (1.0 / replicas)

    advance(1)
    advance(0)
    own = pl.ds(pl.multiple_of(f * width, LANES), width)
    for m in range(2):
        at = slice(m * rank, (m + 1) * rank)
        own_basis[at] = dot32(inv[m], total[at, own], NN) * (1.0 / replicas)


def finish(merged, total, folded, left_in, basis_in, out, left_out, basis_out):
    rank = total.shape[0] // 2
    block = out.shape[2]
    here = pl.ds(pl.multiple_of(pl.program_id(0) * block, block), block)

    @pl.when(pl.program_id(0) == 0)
    def _():
        left_out[...] = left_in[...]
        basis_out[...] = basis_in[...]

    for m in range(2):
        approx = dot32(folded[m], total[m * rank : (m + 1) * rank, here], NN)
        out[m] = merged[m, :, here] - approx


def solution(mesh):
    n, replicas = mesh.shape["fsdp"], mesh.shape["replica"]
    nb, nr = log2(n), log2(replicas)

    def shards(grads, errors, basis):
        _, nmat, rows, cols = grads.shape
        width, _, rank = basis.shape
        grads, errors = grads[0], errors[0]
        basis_t = jnp.transpose(basis, (1, 2, 0)).reshape(nmat * rank, width)
        full = nmat * rank
        share = width // replicas >= LANES
        piece = width // replicas if share else width
        reduce_parts = plan(nb, nr, share)[0]
        nparts, steps = len(reduce_parts), len(reduce_parts[0][2])
        most = max(sum(1 << len(stage) for stage in stages) for _, _, stages in reduce_parts)
        arrivals = max(offsets[-1] for _, _, offsets in layout(nb, nr, cols))
        vmem = pl.BlockSpec(memory_space=pltpu.VMEM)
        hbm = pl.BlockSpec(memory_space=pltpu.HBM)
        dma = pltpu.SemaphoreType.DMA
        merged, total, left_t, own_basis, folded = pl.pallas_call(
            functools.partial(exchange, n, replicas, share),
            out_shape=[
                pltpu.VMEM((nmat, rows, cols), F32),
                pltpu.VMEM((full, cols), F32),
                pltpu.VMEM((full, rows), F32),
                pltpu.VMEM((full, width), F32),
                pltpu.VMEM((nmat, rows, rank), F32),
            ],
            in_specs=[hbm, hbm, vmem],
            out_specs=[vmem] * 5,
            scratch_shapes=[
                pltpu.VMEM((2,) * (nb + nr * share) + (full, piece), F32),
                pltpu.VMEM((nmat, rows, cols), BF16),
                pltpu.VMEM((nmat, 2 * rows, cols), BF16),
                pltpu.VMEM((nmat, 2 * rank, 2 * rows), F32),
                pltpu.VMEM((nr + 1, nmat, rank, 2 * rows), F32),
                pltpu.VMEM((nr, nmat, rank, 2 * rows), F32),
                pltpu.VMEM((full, cols), F32),
                pltpu.VMEM((full, arrivals), F32),
                pltpu.VMEM((steps + 1, rank, LANES), F32),
                pltpu.VMEM((steps, most, rank, LANES), F32),
                dma((nmat, 2)),
                dma((2, 3, most)), dma((2, 3, most)),
                dma((nr, nmat)), dma((nr, nmat)),
                dma((nparts, steps, most)), dma((nparts, steps, most)),
                dma((steps, most)), dma((steps, most)),
                dma((nparts, steps, most)), dma((nparts, steps, most)),
            ],
            compiler_params=pltpu.CompilerParams(
                collective_id=0, has_side_effects=True, vmem_limit_bytes=56 * 1024 * 1024
            ),
        )(grads, errors, basis_t)

        block = 1024
        whole = lambda a: pl.BlockSpec(a.shape, lambda i: (0,) * a.ndim)
        new_errors, left_t, own_basis = pl.pallas_call(
            finish,
            grid=(cols // block,),
            out_shape=[
                jax.ShapeDtypeStruct((nmat, rows, cols), F32),
                jax.ShapeDtypeStruct(left_t.shape, F32),
                jax.ShapeDtypeStruct(own_basis.shape, F32),
            ],
            in_specs=[
                vmem,
                vmem,
                vmem,
                vmem,
                vmem,
            ],
            out_specs=[
                pl.BlockSpec((nmat, rows, block), lambda i: (0, 0, i)),
                whole(left_t),
                whole(own_basis),
            ],
            compiler_params=pltpu.CompilerParams(vmem_limit_bytes=24 * 1024 * 1024),
        )(merged, total, folded, left_t, own_basis)
        left = jnp.transpose(left_t.reshape(nmat, rank, rows), (0, 2, 1))
        new_basis = jnp.transpose(own_basis.reshape(nmat, rank, width), (2, 0, 1))
        return (new_errors[None], left, new_basis)

    in_specs = (
        P("replica", None, "fsdp", None),
        P("replica", None, "fsdp", None),
        P("fsdp", None, None),
    )
    out_specs = (P("replica", None, "fsdp", None), P(None, "fsdp", None), P("fsdp", None, None))
    return jax.shard_map(shards, mesh=mesh, in_specs=in_specs, out_specs=out_specs, check_vma=False)
```

```python
import functools

import jax
import jax.numpy as jnp
from jax import lax
from jax.experimental import pallas as pl
from jax.experimental.pallas import tpu as pltpu
from jax.sharding import PartitionSpec as P

MESH = pl.DeviceIdType.MESH
F32, BF16 = jnp.float32, jnp.bfloat16
TILE = 512
LANES = 128
NT = (((1,), (1,)), ((), ()))
NN = (((1,), (0,)), ((), ()))
TN = (((0,), (0,)), ((), ()))


def split(x):
    high = x.astype(BF16)
    return high, (x - high.astype(F32)).astype(BF16)


def dot32(a, b, dims):
    (ca,), (cb,) = dims[0]
    ah, al = split(a)
    bh, bl = split(b)
    left = jnp.concatenate([ah, ah, al], axis=ca)
    right = jnp.concatenate([bh, bl, bh], axis=cb)
    return lax.dot_general(left, right, dims, preferred_element_type=F32)


def log2(n):
    return n.bit_length() - 1


def plan(nb, nr, share):
    core, near = [("fsdp", 0)], [("fsdp", 1)]
    far = [("fsdp", b) for b in range(2, nb)]
    across = [("replica", b) for b in range(nr)]
    plane_first = [core, near + across, far]
    far_first = [core, far, near + across]
    reduce_parts = [
        (0, 32, plane_first), (32, 40, plane_first), (40, 64, far_first),
    ]
    plane = near + across if share else near
    gather_parts = [(0, 40, [far, plane, core]), (40, 64, [plane, far, core])]
    return reduce_parts, gather_parts


def layout(nb, nr, cols):
    out = []
    for _, _, stages in plan(nb, nr, False)[0]:
        cuts, sizes, offsets = [], [cols], [0]
        for stage in stages:
            members = 1 << len(stage)
            cuts.append(sizes[-1] // members >= LANES)
            sizes.append(sizes[-1] // members if cuts[-1] else sizes[-1])
            offsets.append(offsets[-1] + (members - cuts[-1]) * sizes[-1])
        out.append((cuts, sizes, offsets))
    return out


def exchange(
    n, replicas, share, grads, errors, basis, merged, total, left_t, own_basis, folded,
    held, g_buf, mhl, acc, ft, ft_in, z, z_in, gram, gram_in,
    load_sem, a_send, a_recv, f_send, f_recv, s_send, s_recv, m_send, m_recv, b_send, b_recv,
):
    nb, nr = log2(n), log2(replicas)
    reduce_parts, gather_parts = plan(nb, nr, share)
    rank = basis.shape[0] // 2
    width = basis.shape[1]
    rows = grads.shape[1]
    cols = grads.shape[2]
    y, f = lax.axis_index("replica"), lax.axis_index("fsdp")

    def bit_of(link):
        return lax.rem(lax.div(f if link[0] == "fsdp" else y, 1 << link[1]), 2)

    def index_of(stage, mask=0):
        total_index = 0
        for i, link in enumerate(stage):
            own = bit_of(link)
            total_index = total_index + (1 - own if mask >> i & 1 else own) * (1 << i)
        return total_index

    def partner(stage, mask):
        there = {"replica": y, "fsdp": f}
        for i, link in enumerate(stage):
            if mask >> i & 1:
                there[link[0]] = there[link[0]] + (1 - 2 * bit_of(link)) * (1 << link[1])
        return (there["replica"], there["fsdp"])

    def masks(stage):
        return range(1, 1 << len(stage))

    loads = [
        [
            pltpu.make_async_copy(grads.at[m], g_buf.at[m], load_sem.at[m, 0]),
            pltpu.make_async_copy(errors.at[m], merged.at[m], load_sem.at[m, 1]),
        ]
        for m in range(2)
    ]
    for load in loads[0] + loads[1]:
        load.start()

    barrier = pltpu.get_barrier_semaphore()
    peers = [(stage, mask) for stage in reduce_parts[0][2] for mask in masks(stage)]
    for stage, mask in peers:
        pl.semaphore_signal(barrier, inc=1, device_id=partner(stage, mask), device_id_type=MESH)
    held_links = [("fsdp", b) for b in range(nb - 1, -1, -1)]
    if share:
        held_links += [("replica", b) for b in range(nr - 1, -1, -1)]
    piece = held.shape[-1]
    mine = tuple(bit_of(link) for link in held_links)
    first_column = sum(bit_of(link) * (1 << link[1]) for link in held_links if link[0] == "replica") * piece
    if share:
        held[mine] = basis[:, pl.ds(pl.multiple_of(first_column, LANES), piece)]
    else:
        held[mine] = basis[...]
    pl.semaphore_wait(barrier, len(peers))

    def gather_copy(part, step, at, mask, slot):
        low, high, stages = gather_parts[part]
        ref = held.at[at + (pl.ds(low, high - low), slice(None))]
        copy = pltpu.make_async_remote_copy(
            src_ref=ref, dst_ref=ref,
            send_sem=a_send.at[part, step, slot], recv_sem=a_recv.at[part, step, slot],
            device_id=partner(stages[step], mask), device_id_type=MESH,
        )
        copy.start()
        return copy

    def gather(part, step):
        stages = gather_parts[part][2]
        done = [link for stage in stages[:step] for link in stage]
        at = tuple(slice(None) if link in done else bit_of(link) for link in held_links)
        return [gather_copy(part, step, at, mask, mask - 1) for mask in masks(stages[step])]

    def pass_on(part, mask):
        first_stage, second_stage, _ = gather_parts[part][2]
        at = []
        for link in held_links:
            own = bit_of(link)
            if link in first_stage:
                own = slice(None)
            elif link in second_stage and mask >> second_stage.index(link) & 1:
                own = 1 - own
            at.append(own)
        return gather_copy(part, 2, tuple(at), 1, mask)

    def factor_tiles(m, free, begin):
        end = 1 << len(free)
        group = 8 if begin % 8 == 0 and end % 8 == 0 else 4

        @pl.loop(begin // group, end // group)
        def _(outer):
            summed = 0.0
            for inner in range(group):
                j = outer * group + inner
                bits = []
                for link in held_links:
                    own = bit_of(link)
                    if link in free:
                        flip = lax.rem(lax.div(j, 1 << free.index(link)), 2)
                        own = own + flip * (1 - 2 * own)
                    bits.append(own)
                start = 0
                for link, value in zip(held_links, bits):
                    start = start + value * ((1 << link[1]) * (width if link[0] == "fsdp" else piece))
                here = pl.ds(pl.multiple_of(start, LANES), piece)
                high, low = split(held[tuple(bits) + (pl.ds(m * rank, rank), slice(None))])
                summed = summed + lax.dot_general(
                    jnp.concatenate([high, low], axis=0), mhl[m, :, here], NT, preferred_element_type=F32
                )
            acc[m] += summed

    copies = [gather(part, 0) for part in range(2)]
    acc[...] = jnp.zeros_like(acc)

    def convert(m):
        for load in loads[m]:
            load.wait()

        @pl.loop(0, cols // (2 * TILE))
        def _(t):
            here = pl.ds(pl.multiple_of(t * 2 * TILE, 2 * TILE), 2 * TILE)
            both = g_buf[m, :, here].astype(F32) + merged[m, :, here]
            merged[m, :, here] = both
            high, low = split(both)
            mhl[m, 0:rows, here] = high
            mhl[m, rows : 2 * rows, here] = low

    one, two, three = gather_parts[0][2]

    passed = [[], []]

    def arrive(part, step):
        if step == 0:
            for copy in copies[part]:
                copy.wait()
            copies[part] = gather(part, 1)
            passed[part].append(pass_on(part, 0))
        elif step == 1:
            for mask, copy in enumerate(copies[part], 1):
                copy.wait_recv()
                passed[part].append(pass_on(part, mask))
            for copy in copies[part]:
                copy.wait_send()
        else:
            for copy in passed[part]:
                copy.wait()

    def factor_send(m, b):
        copy = pltpu.make_async_remote_copy(
            src_ref=ft.at[b, m], dst_ref=ft_in.at[b, m],
            send_sem=f_send.at[b, m], recv_sem=f_recv.at[b, m],
            device_id=partner([("replica", b)], 1), device_id_type=MESH,
        )
        copy.start()
        return copy

    def factor_first(m):
        factor_tiles(m, one + two + three, 1 << len(one + two))
        whole = acc[m, 0:rank] + acc[m, rank : 2 * rank]
        single = whole[:, 0:rows] + whole[:, rows : 2 * rows]
        ft[0, m] = jnp.concatenate([single, single], axis=1)
        return factor_send(m, 0)

    def factor_last(m, copy):
        for b in range(nr):
            copy.wait()
            ft[b + 1, m] = ft[b, m] + ft_in[b, m]
            if b + 1 < nr:
                copy = factor_send(m, b + 1)
        return ft[nr, m] * (1.0 / replicas)

    convert(0)
    for part in range(2):
        arrive(part, 0)
    convert(1)
    factor_tiles(0, one, 0)
    for part in range(2):
        arrive(part, 1)
    factor_tiles(0, one + two, 1 << len(one))
    factor_tiles(1, one + two, 0)
    arrive(0, 2)
    f_copies = [factor_first(0)]
    arrive(1, 2)
    f_copies.append(factor_first(1))

    def term(m, start, count):
        high, low = split(factors[m])
        weights = jnp.concatenate([high, low], axis=0)

        @pl.loop(0, count // (4 * TILE))
        def _(t):
            here = pl.ds(pl.multiple_of(start + t * 4 * TILE, 4 * TILE), 4 * TILE)
            out = lax.dot_general(weights, mhl[m, :, here], NN, preferred_element_type=F32)
            z[m * rank : (m + 1) * rank, here] = out[0:rank] + out[rank : 2 * rank]

    half = cols // 2
    core = bit_of(("fsdp", 0))
    parts = range(len(reduce_parts))
    nsteps = 3
    shape = layout(nb, nr, cols)
    starts = [[0] for _ in parts]

    def send(p, step):
        low, high, stages = reduce_parts[p]
        cuts, sizes, offsets = shape[p]
        stage, size, start = stages[step], sizes[step + 1], starts[p][step]
        place = index_of(stage)
        starts[p].append(start + place * size if cuts[step] else start)
        if not cuts[step]:
            own_at = pl.multiple_of(offsets[step] + place * size, LANES)
            z_in[low:high, pl.ds(own_at, size)] = z[low:high, pl.ds(pl.multiple_of(start, LANES), size)]
        out = []
        for mask in masks(stage):
            if cuts[step]:
                away, land = start + index_of(stage, mask) * size, offsets[step] + (mask - 1) * size
            else:
                away, land = start, offsets[step] + place * size
            copy = pltpu.make_async_remote_copy(
                src_ref=z.at[pl.ds(low, high - low), pl.ds(pl.multiple_of(away, LANES), size)],
                dst_ref=z_in.at[pl.ds(low, high - low), pl.ds(pl.multiple_of(land, LANES), size)],
                send_sem=s_send.at[p, step, mask - 1], recv_sem=s_recv.at[p, step, mask - 1],
                device_id=partner(stage, mask), device_id_type=MESH,
            )
            copy.start()
            out.append(copy)
        return out

    def gram_send(step):
        stage = [link for link in reduce_parts[0][2][step] if link[0] == "fsdp"]
        place = index_of(stage)
        gram_in[step, place] = gram[step]
        out = []
        for mask in masks(stage):
            copy = pltpu.make_async_remote_copy(
                src_ref=gram.at[step], dst_ref=gram_in.at[step, place],
                send_sem=m_send.at[step, mask - 1], recv_sem=m_recv.at[step, mask - 1],
                device_id=partner(stage, mask), device_id_type=MESH,
            )
            copy.start()
            out.append(copy)
        return out

    copies = []
    factors = []
    for m in range(2):
        factors.append(factor_last(m, f_copies[m]))
        term(m, (1 - core) * half, half)
        copies += [send(p, 0) for p in parts if reduce_parts[p][0] // rank == m]
    factor = jnp.concatenate(factors, axis=0)
    product = lax.dot_general(
        factor, jnp.concatenate([factor, factor], axis=0), NT,
        precision=lax.Precision.HIGHEST, preferred_element_type=F32,
    ) * 0.5
    lane = lax.broadcasted_iota(jnp.int32, (rank, LANES), 1)
    gram[0] = jnp.where(lane < rank, product[0:rank], product[rank : 2 * rank])
    g_copies = gram_send(0)
    for m in range(2):
        term(m, core * half, half)
    for step in range(nsteps):
        for p in parts:
            low, high, stages = reduce_parts[p]
            cuts, sizes, offsets = shape[p]
            size = sizes[step + 1]
            for copy in copies[p]:
                copy.wait()
            here = pl.ds(pl.multiple_of(starts[p][step + 1], LANES), size)
            members = 1 << len(stages[step])
            terms = [
                z_in[low:high, offsets[step] + i * size : offsets[step] + (i + 1) * size]
                for i in range(members - cuts[step])
            ]
            added = z[low:high, here] + terms[0] if cuts[step] else terms[0]
            for term_in in terms[1:]:
                added = added + term_in
            if step + 1 < nsteps:
                z[low:high, here] = added
                copies[p] = send(p, step + 1)
            else:
                total[low:high, here] = added
        for copy in g_copies:
            copy.wait()
        members = len(g_copies) + 1
        summed = gram_in[step, 0]
        for i in range(1, members):
            summed = summed + gram_in[step, i]
        gram[step + 1] = summed
        g_copies = gram_send(step + 1) if step + 1 < nsteps else []

    def back_copy(p, step, start, size, mask, slot):
        low, high, stages = reduce_parts[p]
        ref = total.at[pl.ds(low, high - low), pl.ds(pl.multiple_of(start, LANES), size)]
        copy = pltpu.make_async_remote_copy(
            src_ref=ref, dst_ref=ref,
            send_sem=b_send.at[p, step, slot], recv_sem=b_recv.at[p, step, slot],
            device_id=partner(stages[step], mask), device_id_type=MESH,
        )
        copy.start()
        return copy

    def back(p, step):
        cuts, sizes, _ = shape[p]
        if not cuts[step]:
            return []
        return [
            back_copy(p, step, starts[p][step + 1], sizes[step + 1], mask, mask - 1)
            for mask in masks(reduce_parts[p][2][step])
        ]

    handed = [[] for _ in parts]

    def advance(step):
        for p in parts:
            sizes, stages = shape[p][1], reduce_parts[p][2]
            if step == 2:
                for copy in copies[p]:
                    copy.wait()
                copies[p] = back(p, 1)
                handed[p].append(back_copy(p, 0, starts[p][2], sizes[2], 1, 0))
            elif step == 1:
                for mask, copy in enumerate(copies[p], 1):
                    copy.wait_recv()
                    start = starts[p][1] + index_of(stages[1], mask) * sizes[2]
                    handed[p].append(back_copy(p, 0, start, sizes[2], 1, mask))
                for copy in copies[p]:
                    copy.wait_send()
            else:
                for copy in handed[p]:
                    copy.wait()

    copies = [back(p, nsteps - 1) for p in parts]

    row = lax.broadcasted_iota(jnp.int32, (rank, LANES), 0)
    lane = lax.broadcasted_iota(jnp.int32, (rank, LANES), 1)
    first = lax.rem(lane, 2 * rank) < rank
    work = jnp.where(lane < 2 * rank, gram[nsteps], jnp.where(lax.rem(lane, rank) == row, 1.0, 0.0))
    for j in range(rank):
        if j == 12:
            advance(2)
        column = jnp.where(first, work[:, j : j + 1], work[:, rank + j : rank + j + 1])
        top = work[j : j + 1, :] / column[j : j + 1, :]
        work = jnp.where(row > j, work - column * top, work)
    pivots = [
        jnp.sum(jnp.where(lane == row + m * rank, work, 0.0), axis=1, keepdims=True) for m in range(2)
    ]
    scaled = work / jnp.sqrt(jnp.where(first, pivots[0], pivots[1]))
    inv = [scaled[:, (2 + m) * rank : (3 + m) * rank] for m in range(2)]
    for m in range(2):
        solved = lax.dot_general(
            inv[m], factor[m * rank : (m + 1) * rank, 0:rows], NN,
            precision=lax.Precision.HIGHEST, preferred_element_type=F32,
        )
        left_t[m * rank : (m + 1) * rank] = solved
        folded[m] = lax.dot_general(
            solved, inv[m], TN, precision=lax.Precision.HIGHEST, preferred_element_type=F32
        ) * (1.0 / replicas)

    advance(1)
    advance(0)
    own = pl.ds(pl.multiple_of(f * width, LANES), width)
    for m in range(2):
        at = slice(m * rank, (m + 1) * rank)
        own_basis[at] = dot32(inv[m], total[at, own], NN) * (1.0 / replicas)


def finish(merged, total, folded, left_in, basis_in, out, left_out, basis_out):
    rank = total.shape[0] // 2
    block = out.shape[2]
    here = pl.ds(pl.multiple_of(pl.program_id(0) * block, block), block)

    @pl.when(pl.program_id(0) == 0)
    def _():
        left_out[...] = left_in[...]
        basis_out[...] = basis_in[...]

    for m in range(2):
        approx = dot32(folded[m], total[m * rank : (m + 1) * rank, here], NN)
        out[m] = merged[m, :, here] - approx


def solution(mesh):
    n, replicas = mesh.shape["fsdp"], mesh.shape["replica"]
    nb, nr = log2(n), log2(replicas)

    def shards(grads, errors, basis):
        _, nmat, rows, cols = grads.shape
        width, _, rank = basis.shape
        grads, errors = grads[0], errors[0]
        basis_t = jnp.transpose(basis, (1, 2, 0)).reshape(nmat * rank, width)
        full = nmat * rank
        share = width // replicas >= LANES
        piece = width // replicas if share else width
        reduce_parts = plan(nb, nr, share)[0]
        nparts, steps = len(reduce_parts), 3
        most = max(1 << len(stage) for stage in reduce_parts[0][2])
        arrivals = max(offsets[-1] for _, _, offsets in layout(nb, nr, cols))
        vmem = pl.BlockSpec(memory_space=pltpu.VMEM)
        hbm = pl.BlockSpec(memory_space=pltpu.HBM)
        dma = pltpu.SemaphoreType.DMA
        merged, total, left_t, own_basis, folded = pl.pallas_call(
            functools.partial(exchange, n, replicas, share),
            out_shape=[
                pltpu.VMEM((nmat, rows, cols), F32),
                pltpu.VMEM((full, cols), F32),
                pltpu.VMEM((full, rows), F32),
                pltpu.VMEM((full, width), F32),
                pltpu.VMEM((nmat, rows, rank), F32),
            ],
            in_specs=[hbm, hbm, vmem],
            out_specs=[vmem] * 5,
            scratch_shapes=[
                pltpu.VMEM((2,) * (nb + nr * share) + (full, piece), F32),
                pltpu.VMEM((nmat, rows, cols), BF16),
                pltpu.VMEM((nmat, 2 * rows, cols), BF16),
                pltpu.VMEM((nmat, 2 * rank, 2 * rows), F32),
                pltpu.VMEM((nr + 1, nmat, rank, 2 * rows), F32),
                pltpu.VMEM((nr, nmat, rank, 2 * rows), F32),
                pltpu.VMEM((full, cols), F32),
                pltpu.VMEM((full, arrivals), F32),
                pltpu.VMEM((steps + 1, rank, LANES), F32),
                pltpu.VMEM((steps, most, rank, LANES), F32),
                dma((nmat, 2)),
                dma((2, 3, most)), dma((2, 3, most)),
                dma((nr, nmat)), dma((nr, nmat)),
                dma((nparts, steps, most)), dma((nparts, steps, most)),
                dma((steps, most)), dma((steps, most)),
                dma((nparts, steps, most)), dma((nparts, steps, most)),
            ],
            compiler_params=pltpu.CompilerParams(
                collective_id=0, has_side_effects=True, vmem_limit_bytes=56 * 1024 * 1024
            ),
        )(grads, errors, basis_t)

        block = 1024
        whole = lambda a: pl.BlockSpec(a.shape, lambda i: (0,) * a.ndim)
        new_errors, left_t, own_basis = pl.pallas_call(
            finish,
            grid=(cols // block,),
            out_shape=[
                jax.ShapeDtypeStruct((nmat, rows, cols), F32),
                jax.ShapeDtypeStruct(left_t.shape, F32),
                jax.ShapeDtypeStruct(own_basis.shape, F32),
            ],
            in_specs=[
                vmem,
                vmem,
                vmem,
                vmem,
                vmem,
            ],
            out_specs=[
                pl.BlockSpec((nmat, rows, block), lambda i: (0, 0, i)),
                whole(left_t),
                whole(own_basis),
            ],
            compiler_params=pltpu.CompilerParams(vmem_limit_bytes=24 * 1024 * 1024),
        )(merged, total, folded, left_t, own_basis)
        left = jnp.transpose(left_t.reshape(nmat, rank, rows), (0, 2, 1))
        new_basis = jnp.transpose(own_basis.reshape(nmat, rank, width), (2, 0, 1))
        return (new_errors[None], left, new_basis)

    in_specs = (
        P("replica", None, "fsdp", None),
        P("replica", None, "fsdp", None),
        P("fsdp", None, None),
    )
    out_specs = (P("replica", None, "fsdp", None), P(None, "fsdp", None), P("fsdp", None, None))
    return jax.shard_map(shards, mesh=mesh, in_specs=in_specs, out_specs=out_specs, check_vma=False)
```

```python
import functools

import jax
import jax.numpy as jnp
from jax import lax
from jax.experimental import pallas as pl
from jax.experimental.pallas import tpu as pltpu
from jax.sharding import PartitionSpec as P

MESH = pl.DeviceIdType.MESH
F32, BF16 = jnp.float32, jnp.bfloat16
TILE = 512
LANES = 128
NT = (((1,), (1,)), ((), ()))
NN = (((1,), (0,)), ((), ()))
TN = (((0,), (0,)), ((), ()))


def split(x):
    high = x.astype(BF16)
    return high, (x - high.astype(F32)).astype(BF16)


def dot32(a, b, dims):
    (ca,), (cb,) = dims[0]
    ah, al = split(a)
    bh, bl = split(b)
    left = jnp.concatenate([ah, ah, al], axis=ca)
    right = jnp.concatenate([bh, bl, bh], axis=cb)
    return lax.dot_general(left, right, dims, preferred_element_type=F32)


def log2(n):
    return n.bit_length() - 1


def plan(nb, nr, share):
    core, near = [("fsdp", 0)], [("fsdp", 1)]
    far = [("fsdp", b) for b in range(2, nb)]
    across = [("replica", b) for b in range(nr)]
    plane_first = [core, near + across, far]
    far_first = [core, far, near + across]
    reduce_parts = [
        (0, 16, plane_first), (16, 32, plane_first), (32, 48, plane_first), (48, 64, far_first),
    ]
    plane = near + across if share else near
    gather_parts = [(0, 40, [far, plane, core]), (40, 64, [plane, far, core])]
    return reduce_parts, gather_parts


def layout(nb, nr, cols):
    out = []
    for _, _, stages in plan(nb, nr, False)[0]:
        cuts, sizes, offsets = [], [cols], [0]
        for stage in stages:
            members = 1 << len(stage)
            cuts.append(sizes[-1] // members >= LANES)
            sizes.append(sizes[-1] // members if cuts[-1] else sizes[-1])
            offsets.append(offsets[-1] + (members - cuts[-1]) * sizes[-1])
        out.append((cuts, sizes, offsets))
    return out


def exchange(
    n, replicas, share, grads, errors, basis, merged, total, left_t, own_basis, folded,
    held, g_buf, mhl, acc, ft, ft_in, z, z_in, gram, gram_in,
    load_sem, a_send, a_recv, f_send, f_recv, s_send, s_recv, m_send, m_recv, b_send, b_recv,
):
    nb, nr = log2(n), log2(replicas)
    reduce_parts, gather_parts = plan(nb, nr, share)
    rank = basis.shape[0] // 2
    width = basis.shape[1]
    rows = grads.shape[1]
    cols = grads.shape[2]
    y, f = lax.axis_index("replica"), lax.axis_index("fsdp")

    def bit_of(link):
        return lax.rem(lax.div(f if link[0] == "fsdp" else y, 1 << link[1]), 2)

    def index_of(stage, mask=0):
        total_index = 0
        for i, link in enumerate(stage):
            own = bit_of(link)
            total_index = total_index + (1 - own if mask >> i & 1 else own) * (1 << i)
        return total_index

    def partner(stage, mask):
        there = {"replica": y, "fsdp": f}
        for i, link in enumerate(stage):
            if mask >> i & 1:
                there[link[0]] = there[link[0]] + (1 - 2 * bit_of(link)) * (1 << link[1])
        return (there["replica"], there["fsdp"])

    def masks(stage):
        return range(1, 1 << len(stage))

    loads = [
        [
            pltpu.make_async_copy(grads.at[m], g_buf.at[m], load_sem.at[m, 0]),
            pltpu.make_async_copy(errors.at[m], merged.at[m], load_sem.at[m, 1]),
        ]
        for m in range(2)
    ]
    for load in loads[0] + loads[1]:
        load.start()

    barrier = pltpu.get_barrier_semaphore()
    peers = [(stage, mask) for stage in reduce_parts[0][2] for mask in masks(stage)]
    for stage, mask in peers:
        pl.semaphore_signal(barrier, inc=1, device_id=partner(stage, mask), device_id_type=MESH)
    held_links = [("fsdp", b) for b in range(nb - 1, -1, -1)]
    if share:
        held_links += [("replica", b) for b in range(nr - 1, -1, -1)]
    piece = held.shape[-1]
    mine = tuple(bit_of(link) for link in held_links)
    first_column = sum(bit_of(link) * (1 << link[1]) for link in held_links if link[0] == "replica") * piece
    if share:
        held[mine] = basis[:, pl.ds(pl.multiple_of(first_column, LANES), piece)]
    else:
        held[mine] = basis[...]
    pl.semaphore_wait(barrier, len(peers))

    def gather_copy(part, step, at, mask, slot):
        low, high, stages = gather_parts[part]
        ref = held.at[at + (pl.ds(low, high - low), slice(None))]
        copy = pltpu.make_async_remote_copy(
            src_ref=ref, dst_ref=ref,
            send_sem=a_send.at[part, step, slot], recv_sem=a_recv.at[part, step, slot],
            device_id=partner(stages[step], mask), device_id_type=MESH,
        )
        copy.start()
        return copy

    def gather(part, step):
        stages = gather_parts[part][2]
        done = [link for stage in stages[:step] for link in stage]
        at = tuple(slice(None) if link in done else bit_of(link) for link in held_links)
        return [gather_copy(part, step, at, mask, mask - 1) for mask in masks(stages[step])]

    def pass_on(part, mask):
        first_stage, second_stage, _ = gather_parts[part][2]
        at = []
        for link in held_links:
            own = bit_of(link)
            if link in first_stage:
                own = slice(None)
            elif link in second_stage and mask >> second_stage.index(link) & 1:
                own = 1 - own
            at.append(own)
        return gather_copy(part, 2, tuple(at), 1, mask)

    def factor_tiles(m, free, begin):
        end = 1 << len(free)
        group = 8 if begin % 8 == 0 and end % 8 == 0 else 4

        @pl.loop(begin // group, end // group)
        def _(outer):
            summed = 0.0
            for inner in range(group):
                j = outer * group + inner
                bits = []
                for link in held_links:
                    own = bit_of(link)
                    if link in free:
                        flip = lax.rem(lax.div(j, 1 << free.index(link)), 2)
                        own = own + flip * (1 - 2 * own)
                    bits.append(own)
                start = 0
                for link, value in zip(held_links, bits):
                    start = start + value * ((1 << link[1]) * (width if link[0] == "fsdp" else piece))
                here = pl.ds(pl.multiple_of(start, LANES), piece)
                high, low = split(held[tuple(bits) + (pl.ds(m * rank, rank), slice(None))])
                summed = summed + lax.dot_general(
                    jnp.concatenate([high, low], axis=0), mhl[m, :, here], NT, preferred_element_type=F32
                )
            acc[m] += summed

    copies = [gather(part, 0) for part in range(2)]
    acc[...] = jnp.zeros_like(acc)

    def convert(m):
        for load in loads[m]:
            load.wait()

        @pl.loop(0, cols // (2 * TILE))
        def _(t):
            here = pl.ds(pl.multiple_of(t * 2 * TILE, 2 * TILE), 2 * TILE)
            both = g_buf[m, :, here].astype(F32) + merged[m, :, here]
            merged[m, :, here] = both
            high, low = split(both)
            mhl[m, 0:rows, here] = high
            mhl[m, rows : 2 * rows, here] = low

    one, two, three = gather_parts[0][2]

    passed = [[], []]

    def arrive(part, step):
        if step == 0:
            for copy in copies[part]:
                copy.wait()
            copies[part] = gather(part, 1)
            passed[part].append(pass_on(part, 0))
        elif step == 1:
            for mask, copy in enumerate(copies[part], 1):
                copy.wait_recv()
                passed[part].append(pass_on(part, mask))
            for copy in copies[part]:
                copy.wait_send()
        else:
            for copy in passed[part]:
                copy.wait()

    def factor_send(m, b):
        copy = pltpu.make_async_remote_copy(
            src_ref=ft.at[b, m], dst_ref=ft_in.at[b, m],
            send_sem=f_send.at[b, m], recv_sem=f_recv.at[b, m],
            device_id=partner([("replica", b)], 1), device_id_type=MESH,
        )
        copy.start()
        return copy

    def factor_first(m):
        factor_tiles(m, one + two + three, 1 << len(one + two))
        whole = acc[m, 0:rank] + acc[m, rank : 2 * rank]
        single = whole[:, 0:rows] + whole[:, rows : 2 * rows]
        ft[0, m] = jnp.concatenate([single, single], axis=1)
        return factor_send(m, 0)

    def factor_last(m, copy):
        for b in range(nr):
            copy.wait()
            ft[b + 1, m] = ft[b, m] + ft_in[b, m]
            if b + 1 < nr:
                copy = factor_send(m, b + 1)
        return ft[nr, m] * (1.0 / replicas)

    convert(0)
    for part in range(2):
        arrive(part, 0)
    convert(1)
    factor_tiles(0, one, 0)
    for part in range(2):
        arrive(part, 1)
    factor_tiles(0, one + two, 1 << len(one))
    factor_tiles(1, one + two, 0)
    arrive(0, 2)
    f_copies = [factor_first(0)]
    arrive(1, 2)
    f_copies.append(factor_first(1))

    def term(m, start, count):
        high, low = split(factors[m])
        weights = jnp.concatenate([high, low], axis=0)

        @pl.loop(0, count // (4 * TILE))
        def _(t):
            here = pl.ds(pl.multiple_of(start + t * 4 * TILE, 4 * TILE), 4 * TILE)
            out = lax.dot_general(weights, mhl[m, :, here], NN, preferred_element_type=F32)
            z[m * rank : (m + 1) * rank, here] = out[0:rank] + out[rank : 2 * rank]

    half = cols // 2
    core = bit_of(("fsdp", 0))
    parts = range(len(reduce_parts))
    nsteps = 3
    shape = layout(nb, nr, cols)
    starts = [[0] for _ in parts]

    def send(p, step):
        low, high, stages = reduce_parts[p]
        cuts, sizes, offsets = shape[p]
        stage, size, start = stages[step], sizes[step + 1], starts[p][step]
        place = index_of(stage)
        starts[p].append(start + place * size if cuts[step] else start)
        if not cuts[step]:
            own_at = pl.multiple_of(offsets[step] + place * size, LANES)
            z_in[low:high, pl.ds(own_at, size)] = z[low:high, pl.ds(pl.multiple_of(start, LANES), size)]
        out = []
        for mask in masks(stage):
            if cuts[step]:
                away, land = start + index_of(stage, mask) * size, offsets[step] + (mask - 1) * size
            else:
                away, land = start, offsets[step] + place * size
            copy = pltpu.make_async_remote_copy(
                src_ref=z.at[pl.ds(low, high - low), pl.ds(pl.multiple_of(away, LANES), size)],
                dst_ref=z_in.at[pl.ds(low, high - low), pl.ds(pl.multiple_of(land, LANES), size)],
                send_sem=s_send.at[p, step, mask - 1], recv_sem=s_recv.at[p, step, mask - 1],
                device_id=partner(stage, mask), device_id_type=MESH,
            )
            copy.start()
            out.append(copy)
        return out

    def gram_send(step):
        stage = [link for link in reduce_parts[0][2][step] if link[0] == "fsdp"]
        place = index_of(stage)
        gram_in[step, place] = gram[step]
        out = []
        for mask in masks(stage):
            copy = pltpu.make_async_remote_copy(
                src_ref=gram.at[step], dst_ref=gram_in.at[step, place],
                send_sem=m_send.at[step, mask - 1], recv_sem=m_recv.at[step, mask - 1],
                device_id=partner(stage, mask), device_id_type=MESH,
            )
            copy.start()
            out.append(copy)
        return out

    copies = []
    factors = []
    for m in range(2):
        factors.append(factor_last(m, f_copies[m]))
        term(m, (1 - core) * half, half)
        copies += [send(p, 0) for p in parts if reduce_parts[p][0] // rank == m]
    factor = jnp.concatenate(factors, axis=0)
    product = lax.dot_general(
        factor, jnp.concatenate([factor, factor], axis=0), NT,
        precision=lax.Precision.HIGHEST, preferred_element_type=F32,
    ) * 0.5
    lane = lax.broadcasted_iota(jnp.int32, (rank, LANES), 1)
    gram[0] = jnp.where(lane < rank, product[0:rank], product[rank : 2 * rank])
    g_copies = gram_send(0)
    for m in range(2):
        term(m, core * half, half)
    for step in range(nsteps):
        for p in parts:
            low, high, stages = reduce_parts[p]
            cuts, sizes, offsets = shape[p]
            size = sizes[step + 1]
            for copy in copies[p]:
                copy.wait()
            here = pl.ds(pl.multiple_of(starts[p][step + 1], LANES), size)
            members = 1 << len(stages[step])
            terms = [
                z_in[low:high, offsets[step] + i * size : offsets[step] + (i + 1) * size]
                for i in range(members - cuts[step])
            ]
            added = z[low:high, here] + terms[0] if cuts[step] else terms[0]
            for term_in in terms[1:]:
                added = added + term_in
            if step + 1 < nsteps:
                z[low:high, here] = added
                copies[p] = send(p, step + 1)
            else:
                total[low:high, here] = added
        for copy in g_copies:
            copy.wait()
        members = len(g_copies) + 1
        summed = gram_in[step, 0]
        for i in range(1, members):
            summed = summed + gram_in[step, i]
        gram[step + 1] = summed
        g_copies = gram_send(step + 1) if step + 1 < nsteps else []

    def back_copy(p, step, start, size, mask, slot):
        low, high, stages = reduce_parts[p]
        ref = total.at[pl.ds(low, high - low), pl.ds(pl.multiple_of(start, LANES), size)]
        copy = pltpu.make_async_remote_copy(
            src_ref=ref, dst_ref=ref,
            send_sem=b_send.at[p, step, slot], recv_sem=b_recv.at[p, step, slot],
            device_id=partner(stages[step], mask), device_id_type=MESH,
        )
        copy.start()
        return copy

    def back(p, step):
        cuts, sizes, _ = shape[p]
        if not cuts[step]:
            return []
        return [
            back_copy(p, step, starts[p][step + 1], sizes[step + 1], mask, mask - 1)
            for mask in masks(reduce_parts[p][2][step])
        ]

    handed = [[] for _ in parts]

    def advance(step):
        for p in parts:
            sizes, stages = shape[p][1], reduce_parts[p][2]
            if step == 2:
                for copy in copies[p]:
                    copy.wait()
                copies[p] = back(p, 1)
                handed[p].append(back_copy(p, 0, starts[p][2], sizes[2], 1, 0))
            elif step == 1:
                for mask, copy in enumerate(copies[p], 1):
                    copy.wait_recv()
                    start = starts[p][1] + index_of(stages[1], mask) * sizes[2]
                    handed[p].append(back_copy(p, 0, start, sizes[2], 1, mask))
                for copy in copies[p]:
                    copy.wait_send()
            else:
                for copy in handed[p]:
                    copy.wait()

    copies = [back(p, nsteps - 1) for p in parts]

    row = lax.broadcasted_iota(jnp.int32, (rank, LANES), 0)
    lane = lax.broadcasted_iota(jnp.int32, (rank, LANES), 1)
    first = lax.rem(lane, 2 * rank) < rank
    work = jnp.where(lane < 2 * rank, gram[nsteps], jnp.where(lax.rem(lane, rank) == row, 1.0, 0.0))
    for j in range(rank):
        if j == 12:
            advance(2)
        column = jnp.where(first, work[:, j : j + 1], work[:, rank + j : rank + j + 1])
        top = work[j : j + 1, :] / column[j : j + 1, :]
        work = jnp.where(row > j, work - column * top, work)
    pivots = [
        jnp.sum(jnp.where(lane == row + m * rank, work, 0.0), axis=1, keepdims=True) for m in range(2)
    ]
    scaled = work / jnp.sqrt(jnp.where(first, pivots[0], pivots[1]))
    inv = [scaled[:, (2 + m) * rank : (3 + m) * rank] for m in range(2)]
    for m in range(2):
        solved = lax.dot_general(
            inv[m], factor[m * rank : (m + 1) * rank, 0:rows], NN,
            precision=lax.Precision.HIGHEST, preferred_element_type=F32,
        )
        left_t[m * rank : (m + 1) * rank] = solved
        folded[m] = lax.dot_general(
            solved, inv[m], TN, precision=lax.Precision.HIGHEST, preferred_element_type=F32
        ) * (1.0 / replicas)

    advance(1)
    advance(0)
    own = pl.ds(pl.multiple_of(f * width, LANES), width)
    for m in range(2):
        at = slice(m * rank, (m + 1) * rank)
        own_basis[at] = dot32(inv[m], total[at, own], NN) * (1.0 / replicas)


def finish(merged, total, folded, left_in, basis_in, out, left_out, basis_out):
    rank = total.shape[0] // 2
    block = out.shape[2]
    here = pl.ds(pl.multiple_of(pl.program_id(0) * block, block), block)

    @pl.when(pl.program_id(0) == 0)
    def _():
        left_out[...] = left_in[...]
        basis_out[...] = basis_in[...]

    for m in range(2):
        approx = dot32(folded[m], total[m * rank : (m + 1) * rank, here], NN)
        out[m] = merged[m, :, here] - approx


def solution(mesh):
    n, replicas = mesh.shape["fsdp"], mesh.shape["replica"]
    nb, nr = log2(n), log2(replicas)

    def shards(grads, errors, basis):
        _, nmat, rows, cols = grads.shape
        width, _, rank = basis.shape
        grads, errors = grads[0], errors[0]
        basis_t = jnp.transpose(basis, (1, 2, 0)).reshape(nmat * rank, width)
        full = nmat * rank
        share = width // replicas >= LANES
        piece = width // replicas if share else width
        reduce_parts = plan(nb, nr, share)[0]
        nparts, steps = len(reduce_parts), 3
        most = max(1 << len(stage) for stage in reduce_parts[0][2])
        arrivals = max(offsets[-1] for _, _, offsets in layout(nb, nr, cols))
        vmem = pl.BlockSpec(memory_space=pltpu.VMEM)
        hbm = pl.BlockSpec(memory_space=pltpu.HBM)
        dma = pltpu.SemaphoreType.DMA
        merged, total, left_t, own_basis, folded = pl.pallas_call(
            functools.partial(exchange, n, replicas, share),
            out_shape=[
                pltpu.VMEM((nmat, rows, cols), F32),
                pltpu.VMEM((full, cols), F32),
                pltpu.VMEM((full, rows), F32),
                pltpu.VMEM((full, width), F32),
                pltpu.VMEM((nmat, rows, rank), F32),
            ],
            in_specs=[hbm, hbm, vmem],
            out_specs=[vmem] * 5,
            scratch_shapes=[
                pltpu.VMEM((2,) * (nb + nr * share) + (full, piece), F32),
                pltpu.VMEM((nmat, rows, cols), BF16),
                pltpu.VMEM((nmat, 2 * rows, cols), BF16),
                pltpu.VMEM((nmat, 2 * rank, 2 * rows), F32),
                pltpu.VMEM((nr + 1, nmat, rank, 2 * rows), F32),
                pltpu.VMEM((nr, nmat, rank, 2 * rows), F32),
                pltpu.VMEM((full, cols), F32),
                pltpu.VMEM((full, arrivals), F32),
                pltpu.VMEM((steps + 1, rank, LANES), F32),
                pltpu.VMEM((steps, most, rank, LANES), F32),
                dma((nmat, 2)),
                dma((2, 3, most)), dma((2, 3, most)),
                dma((nr, nmat)), dma((nr, nmat)),
                dma((nparts, steps, most)), dma((nparts, steps, most)),
                dma((steps, most)), dma((steps, most)),
                dma((nparts, steps, most)), dma((nparts, steps, most)),
            ],
            compiler_params=pltpu.CompilerParams(
                collective_id=0, has_side_effects=True, vmem_limit_bytes=56 * 1024 * 1024
            ),
        )(grads, errors, basis_t)

        block = 2048
        whole = lambda a: pl.BlockSpec(a.shape, lambda i: (0,) * a.ndim)
        new_errors, left_t, own_basis = pl.pallas_call(
            finish,
            grid=(cols // block,),
            out_shape=[
                jax.ShapeDtypeStruct((nmat, rows, cols), F32),
                jax.ShapeDtypeStruct(left_t.shape, F32),
                jax.ShapeDtypeStruct(own_basis.shape, F32),
            ],
            in_specs=[
                vmem,
                vmem,
                vmem,
                vmem,
                vmem,
            ],
            out_specs=[
                pl.BlockSpec((nmat, rows, block), lambda i: (0, 0, i)),
                whole(left_t),
                whole(own_basis),
            ],
            compiler_params=pltpu.CompilerParams(vmem_limit_bytes=24 * 1024 * 1024),
        )(merged, total, folded, left_t, own_basis)
        left = jnp.transpose(left_t.reshape(nmat, rank, rows), (0, 2, 1))
        new_basis = jnp.transpose(own_basis.reshape(nmat, rank, width), (2, 0, 1))
        return (new_errors[None], left, new_basis)

    in_specs = (
        P("replica", None, "fsdp", None),
        P("replica", None, "fsdp", None),
        P("fsdp", None, None),
    )
    out_specs = (P("replica", None, "fsdp", None), P(None, "fsdp", None), P("fsdp", None, None))
    return jax.shard_map(shards, mesh=mesh, in_specs=in_specs, out_specs=out_specs, check_vma=False)
```
